32 devices in a mesh: tm: 2 (over x), height: 16 (over z, y, core).
Axes of the slice: x: 2, y: 2, z: 4, core: 2. Of those that a mesh axis runs over, the one named last changes fastest.
Arguments:
- inputs: bfloat16 [4, 384, 4, 1024], P('tm', 'height'), may hold values from -24 to 24
- w_query: bfloat16 [1024, 1024], replicated, may hold values from -0.1875 to 0.1875
- w_key: bfloat16 [1024, 1024], replicated, may hold values from -0.1875 to 0.1875
- w_value: bfloat16 [1024, 1024], replicated, may hold values from -0.1875 to 0.1875
- w_out: bfloat16 [1024, 1024], replicated, may hold values from -0.1875 to 0.1875
- grad_out: bfloat16 [4, 384, 4, 1024], P('tm', 'height'), may hold values from -6 to 6
Outputs:
- attended: bfloat16 [4, 384, 4, 1024], P('tm', 'height')
- grad_in: bfloat16 [4, 384, 4, 1024], P('tm', 'height')
The draws below stay inside these ranges and needn't reach their ends.
All inputs are finite; a program needn't handle non-finite values.
Results may differ from the reference program's by a relative error of at most 0.03.
The reference program's roundings to bfloat16 on the way count: a program that leaves them out, or rounds other values in their place, can miss the bound.
Values may be sent and summed in bfloat16 or wider, within the bound.
A program may use at most 128 MiB of HBM per device.

```python
import jax
import jax.numpy as jnp
from jax import lax

D = 1024
HD = 64
RT = 2
RH = 7
RW = 7
HB = 24
WC = 4
NT = 4
NH = 384


def draw_inputs(key, part):
    key = jax.random.fold_in(key, 11)
    shape = (NT, NH, WC, D)
    values = jnp.clip(jax.random.normal(key, shape, jnp.float32), -6.0, 6.0)
    return values.astype(jnp.bfloat16)


def levels(key, shape, cuts, least, largest):
    level, own = 1.0, jax.random.fold_in(key, 6)
    for position, parts in cuts:
        draws = jnp.exp(jax.random.uniform(jax.random.fold_in(own, position), (parts,), jnp.float32, least / len(cuts), largest / len(cuts)))
        level = level * jnp.repeat(draws, shape[position] // parts).reshape([-1 if axis == position else 1 for axis in range(len(shape))])
    return level


def noise(rng, dims, scale, limit, pieces=(), kind=jnp.bfloat16):
    entries = jax.random.normal(rng, dims, jnp.float32) * scale
    if len(pieces) > 0:
        entries = levels(rng, dims, pieces, -0.22, 0.18) * entries
    return jnp.clip(entries, min=-limit, max=limit).astype(kind)


def setup_inputs(seed: int = 0) -> dict:
    arg_keys = jax.random.split(jax.random.key(seed), 7)
    inputs = draw_inputs(jax.random.fold_in(arg_keys[6], 71), 0)
    w_query = noise(arg_keys[1], (D, D), D ** -0.5, 0.1875)
    w_key = noise(arg_keys[2], (D, D), D ** -0.5, 0.1875)
    w_value = noise(arg_keys[3], (D, D), D ** -0.5, 0.1875)
    w_out = noise(arg_keys[4], (D, D), D ** -0.5, 0.1875)
    grad_out = noise(arg_keys[5], (NT, NH, WC, D), 1.0, 6.0, ((0, 2), (1, 16)))
    return {"inputs": inputs, "w_query": w_query, "w_key": w_key, "w_value": w_value, "w_out": w_out, "grad_out": grad_out}


def attend(queries, keyvals, grads, allowed):
    qcount = queries.shape[0]
    kcount = keyvals.shape[0]
    width = queries.shape[1]
    heads = width // HD
    scale = HD ** -0.5
    qh = queries.reshape(qcount, heads, HD).astype(jnp.float32)
    kh = keyvals[:, :width].reshape(kcount, heads, HD).astype(jnp.float32)
    vh = keyvals[:, width:].reshape(kcount, heads, HD).astype(jnp.float32)
    scores = jnp.einsum("qhd,khd->hqk", qh, kh) * scale
    scores = jnp.where(allowed[None], scores, jnp.float32(-1e30))
    top = jnp.max(scores, axis=2, keepdims=True)
    expo = jnp.exp(scores - top)
    probs = expo / jnp.sum(expo, axis=2, keepdims=True)
    probs_b = probs.astype(jnp.bfloat16)
    mixed = jnp.einsum("hqk,khd->qhd", probs_b.astype(jnp.float32), vh).astype(jnp.bfloat16)
    gh = grads.reshape(qcount, heads, HD).astype(jnp.float32)
    delta = jnp.sum(gh * mixed.astype(jnp.float32), axis=2).T
    dprob = jnp.einsum("qhd,khd->hqk", gh, vh)
    dscore = (probs * (dprob - delta[:, :, None]) * scale).astype(jnp.bfloat16).astype(jnp.float32)
    grad_q = jnp.einsum("hqk,khd->qhd", dscore, kh).astype(jnp.bfloat16)
    grad_k = jnp.einsum("hqk,qhd->khd", dscore, qh)
    grad_v = jnp.einsum("hqk,qhd->khd", probs_b.astype(jnp.float32), gh)
    both = jnp.concatenate([grad_k.reshape(kcount, width), grad_v.reshape(kcount, width)], axis=1)
    return mixed.reshape(qcount, width), grad_q.reshape(qcount, width), both


def reference(inputs, w_query, w_key, w_value, w_out, grad_out):
    tokens = inputs.reshape(-1, D)
    query = jnp.dot(tokens, w_query, preferred_element_type=jnp.float32).astype(jnp.bfloat16).reshape(NT, NH, WC, D)
    key = jnp.dot(tokens, w_key, preferred_element_type=jnp.float32).astype(jnp.bfloat16).reshape(NT, NH, WC, D)
    value = jnp.dot(tokens, w_value, preferred_element_type=jnp.float32).astype(jnp.bfloat16).reshape(NT, NH, WC, D)
    grad_att = jnp.dot(grad_out.reshape(-1, D), w_out.T, preferred_element_type=jnp.float32).astype(jnp.bfloat16).reshape(NT, NH, WC, D)
    keyval = jnp.concatenate([key, value], axis=3)
    keyval = jnp.pad(keyval, ((RT, RT), (RH, RH), (0, 0), (0, 0)))
    frame_ok = jnp.pad(jnp.ones((NT,), jnp.int32), (RT, RT))
    row_ok = jnp.pad(jnp.ones((NH,), jnp.int32), (RH, RH))
    qrow = jnp.repeat(jnp.arange(HB), WC)
    qcol = jnp.tile(jnp.arange(WC), HB)
    krow = jnp.repeat(jnp.arange(HB + 2 * RH), WC)
    kcol = jnp.tile(jnp.arange(WC), HB + 2 * RH)
    rdiff = krow[None, :] - qrow[:, None]
    base = (rdiff >= 0) & (rdiff <= 2 * RH) & (jnp.abs(kcol[None, :] - qcol[:, None]) <= RW)
    bands = NH // HB
    span_f = 2 * RT + 1
    span_r = HB + 2 * RH

    def step(carry, index):
        frame = index // bands
        row0 = (index % bands) * HB
        zero = jnp.int32(0)
        qb = lax.dynamic_slice(query, (frame, row0, zero, zero), (1, HB, WC, D)).reshape(HB * WC, D)
        gb = lax.dynamic_slice(grad_att, (frame, row0, zero, zero), (1, HB, WC, D)).reshape(HB * WC, D)
        kvb = lax.dynamic_slice(keyval, (frame, row0, zero, zero), (span_f, span_r, WC, 2 * D))
        fok = lax.dynamic_slice(frame_ok, (frame,), (span_f,)) > 0
        rok = lax.dynamic_slice(row_ok, (row0,), (span_r,)) > 0
        kok = jnp.repeat(rok, WC)
        allowed = base[:, None, :] & kok[None, None, :] & fok[None, :, None]
        allowed = allowed.reshape(HB * WC, span_f * span_r * WC)
        mixed, grad_q, both = attend(qb, kvb.reshape(-1, 2 * D), gb, allowed)
        old = lax.dynamic_slice(carry, (frame, row0, zero, zero), (span_f, span_r, WC, 2 * D))
        carry = lax.dynamic_update_slice(carry, old + both.reshape(span_f, span_r, WC, 2 * D), (frame, row0, zero, zero))
        return carry, (mixed, grad_q)

    start = jnp.zeros((NT + 2 * RT, NH + 2 * RH, WC, 2 * D), jnp.float32)
    total, (mixed_all, gradq_all) = lax.scan(step, start, jnp.arange(NT * bands, dtype=jnp.int32))
    mixed_all = mixed_all.reshape(NT, NH, WC, D)
    gradq_all = gradq_all.reshape(NT, NH, WC, D)
    attended = jnp.dot(mixed_all.reshape(-1, D), w_out, preferred_element_type=jnp.float32).astype(jnp.bfloat16).reshape(NT, NH, WC, D)
    core = total[RT:RT + NT, RH:RH + NH]
    grad_key = core[..., :D].astype(jnp.bfloat16).reshape(-1, D)
    grad_value = core[..., D:].astype(jnp.bfloat16).reshape(-1, D)
    grad_in = jnp.dot(gradq_all.reshape(-1, D), w_query.T, preferred_element_type=jnp.float32)
    grad_in = grad_in + jnp.dot(grad_key, w_key.T, preferred_element_type=jnp.float32)
    grad_in = grad_in + jnp.dot(grad_value, w_value.T, preferred_element_type=jnp.float32)
    return attended, grad_in.astype(jnp.bfloat16).reshape(NT, NH, WC, D)
```

```python
import functools

import jax
import jax.numpy as jnp
from jax import lax
from jax.experimental import pallas as pl
from jax.experimental.pallas import tpu as pltpu
from jax.sharding import PartitionSpec as P

HD = 64
RT = 2
RH = 7
RW = 7
PAD = 8
BR = 8
NHG = 4
BF = jnp.bfloat16
F32 = jnp.float32


def dot_nn(a, b):
    return jnp.dot(a, b, preferred_element_type=F32)


def dot_nt(a, b):
    return lax.dot_general(a, b, (((1,), (1,)), ((), ())), preferred_element_type=F32)


def stack_heads(a):
    head = lax.broadcasted_iota(jnp.int32, a.shape, 1) // HD
    return jnp.concatenate([jnp.where(head == h, a, jnp.zeros_like(a)) for h in range(NHG)], axis=0)


def pick_heads(a):
    n = a.shape[0] // NHG
    head = lax.broadcasted_iota(jnp.int32, (n, a.shape[1]), 1) // HD
    out = a[:n]
    for h in range(1, NHG):
        out = jnp.where(head == h, a[h * n : (h + 1) * n], out)
    return out


def make_bias(block, dims):
    frames, rows, cols, slots, tm_size, height_size = dims
    t = lax.axis_index("tm")
    first = lax.axis_index("height") * rows
    span = (BR + 2 * PAD) * cols
    own = BR * cols
    shape = (frames * own, slots * span)
    i = lax.broadcasted_iota(jnp.int32, shape, 0)
    j = lax.broadcasted_iota(jnp.int32, shape, 1)
    qf = t * frames + i // own
    qr = (i % own) // cols
    slot = j // span
    kr = (j % span) // cols
    group = slot // frames
    if slots == 2 * frames:
        base = jnp.where(group == 0, t, 1 - t)
    else:
        base = jnp.where(group == 0, t, jnp.where(group == 1, t - 1, t + 1))
    kf = base * frames + slot % frames
    near = (jnp.abs(kf - qf) <= RT) & (jnp.abs(kr - PAD - qr) <= RH)
    row = first + block * BR + kr - PAD
    real = (kf >= 0) & (kf < tm_size * frames) & (row >= 0) & (row < height_size * rows)
    return jnp.where(near & real, 0.0, -1e30).astype(F32)


def forward_block(b, g, dims, q_ref, k_ref, v_ref, g_ref, mixed_ref, dq_ref, stat_ref, bias_ref):
    frames, rows, cols, slots, _, _ = dims
    own = BR * cols
    span = (BR + 2 * PAD) * cols
    width = NHG * HD
    at = pl.ds(g * width, width)
    mine = pl.ds(pl.multiple_of((b + 1) * own, own), own)
    inner = pl.ds(pl.multiple_of(b * own, own), own)
    wide = pl.ds(pl.multiple_of(b * own, own), span)
    q = stack_heads(q_ref[:frames, mine, at].reshape(frames * own, width))
    gr = stack_heads(g_ref[:frames, mine, at].reshape(frames * own, width))
    k = k_ref[:, wide, at].reshape(slots * span, width)
    v = v_ref[:, wide, at].reshape(slots * span, width)
    n = frames * own
    scale = HD ** (-0.5)
    s = dot_nt(q, k) * scale
    s = (s.reshape(NHG, n, slots * span) + bias_ref[...][None]).reshape(NHG * n, slots * span)
    top = jnp.max(s, axis=1, keepdims=True)
    e = jnp.exp(s - top)
    total = jnp.sum(e, axis=1, keepdims=True)
    p = e * (1.0 / total)
    mixed = dot_nn(p.astype(BF), v).astype(BF)
    delta = jnp.sum(gr.astype(F32) * mixed.astype(F32), axis=1, keepdims=True)
    dp = dot_nt(gr, v)
    ds = (p * ((dp - delta) * scale)).astype(BF)
    dq = dot_nn(ds, k)
    mixed_ref[:, inner, at] = pick_heads(mixed).reshape(frames, own, width)
    dq_ref[:, inner, at] = pick_heads(dq).astype(BF).reshape(frames, own, width)
    lse = top + jnp.log(total)
    lane = lax.broadcasted_iota(jnp.int32, (n, 128), 1)
    stat = stat_ref[:, inner, :].reshape(n, 128)
    for h in range(NHG):
        stat = jnp.where(lane == g * NHG + h, lse[h * n : (h + 1) * n], stat)
        stat = jnp.where(lane == 64 + g * NHG + h, delta[h * n : (h + 1) * n], stat)
    stat_ref[:, inner, :] = stat.reshape(frames, own, 128)


def backward_block(b, g, dims, q_ref, k_ref, v_ref, g_ref, dk_ref, dv_ref, flip_ref, bias_ref):
    frames, rows, cols, slots, _, _ = dims
    own = BR * cols
    span = (BR + 2 * PAD) * cols
    width = NHG * HD
    at = pl.ds(g * width, width)
    mine = pl.ds(pl.multiple_of((b + 1) * own, own), own)
    inner = pl.ds(pl.multiple_of(b * own, own), own)
    wide = pl.ds(pl.multiple_of(b * own, own), span)
    k = stack_heads(k_ref[:frames, mine, at].reshape(frames * own, width))
    v = stack_heads(v_ref[:frames, mine, at].reshape(frames * own, width))
    q = q_ref[:, wide, at].reshape(slots * span, width)
    gr = g_ref[:, wide, at].reshape(slots * span, width)
    n = frames * own
    full = (NHG, n, slots * span)
    scale = HD ** (-0.5)
    lse = flip_ref[g * NHG : (g + 1) * NHG, :]
    delta = flip_ref[64 + g * NHG : 64 + (g + 1) * NHG, :]
    s = dot_nt(k, q).reshape(full) * scale
    p = jnp.exp(s + bias_ref[...][None] - lse[:, None, :])
    dv = dot_nn(p.astype(BF).reshape(NHG * n, -1), gr)
    dp = dot_nt(v, gr).reshape(full)
    ds = (p * ((dp - delta[:, None, :]) * scale)).astype(BF)
    dk = dot_nn(ds.reshape(NHG * n, -1), q)
    dk_ref[:, inner, at] = pick_heads(dk).astype(BF).reshape(frames, own, width)
    dv_ref[:, inner, at] = pick_heads(dv).astype(BF).reshape(frames, own, width)


def project(src_ref, w_ref, dst_ref, slots, flip):
    width = w_ref.shape[0]
    tile = 256

    def tile_step(i, _):
        at = pl.ds(pl.multiple_of(i * tile, tile), tile)

        def slot_step(s, _):
            if flip:
                out = dot_nt(src_ref[s], w_ref[at, :])
            else:
                out = dot_nn(src_ref[s], w_ref[:, at])
            dst_ref[s, :, at] = out.astype(BF)
            return 0

        return lax.fori_loop(slots[0], slots[1], slot_step, 0)

    lax.fori_loop(0, width // tile, tile_step, 0)


def first_kernel(
    dims, x_ref, go_ref, wq_ref, wk_ref, wv_ref, wo_ref,
    attended_ref, dq_ref, stat_ref, k_ref, v_ref, q_ref, g_ref, mixed_ref, bias_ref,
):
    frames, rows, cols, slots, _, _ = dims
    project(x_ref, wq_ref, q_ref, (0, frames), False)
    project(go_ref, wo_ref, g_ref, (0, frames), True)
    project(x_ref, wk_ref, k_ref, (0, slots), False)
    project(x_ref, wv_ref, v_ref, (0, slots), False)
    stat_ref[...] = jnp.zeros_like(stat_ref)

    def step(b, _):
        bias_ref[...] = make_bias(b, dims)
        for g in range(x_ref.shape[2] // (NHG * HD)):
            forward_block(b, g, dims, q_ref, k_ref, v_ref, g_ref, mixed_ref, dq_ref, stat_ref, bias_ref)
        return 0

    lax.fori_loop(0, rows // BR, step, 0)
    project(mixed_ref, wo_ref, attended_ref, (0, frames), False)


def second_kernel(
    dims, x_ref, go_ref, wq_ref, wk_ref, wv_ref, wo_ref, k_ref, v_ref, dq_ref, stat_ref,
    out_ref, q_ref, g_ref, dk_ref, dv_ref, bias_ref, flip_ref,
):
    frames, rows, cols, slots, _, _ = dims
    own = BR * cols
    span = (BR + 2 * PAD) * cols
    project(x_ref, wq_ref, q_ref, (0, slots), False)
    project(go_ref, wo_ref, g_ref, (0, slots), True)

    def step(b, _):
        bias_ref[...] = make_bias(b, dims)
        stat = stat_ref[:, pl.ds(pl.multiple_of(b * own, own), span), :]
        flip_ref[...] = stat.reshape(slots * span, 128).T
        for g in range(x_ref.shape[2] // (NHG * HD)):
            backward_block(b, g, dims, q_ref, k_ref, v_ref, g_ref, dk_ref, dv_ref, flip_ref, bias_ref)
        return 0

    lax.fori_loop(0, rows // BR, step, 0)
    tile = 256

    def out_step(i, _):
        at = pl.ds(pl.multiple_of(i * tile, tile), tile)
        for f in range(frames):
            total = dot_nt(dq_ref[f], wq_ref[at, :])
            total += dot_nt(dk_ref[f], wk_ref[at, :])
            total += dot_nt(dv_ref[f], wv_ref[at, :])
            out_ref[f, :, at] = total.astype(BF)
        return 0

    lax.fori_loop(0, x_ref.shape[2] // tile, out_step, 0)


def around(block, edge):
    tm, height = lax.axis_size("tm"), lax.axis_size("height")
    if tm == 2:
        groups = [block, lax.ppermute(block, "tm", [(0, 1), (1, 0)])]
    else:
        up = [(i, i + 1) for i in range(tm - 1)]
        groups = [block, lax.ppermute(block, "tm", up), lax.ppermute(block, "tm", [(b, a) for a, b in up])]
    wide = jnp.concatenate(groups, axis=0)
    up = [(i, i + 1) for i in range(height - 1)]
    low = lax.ppermute(wide[:, -edge:], "height", up)
    high = lax.ppermute(wide[:, :edge], "height", [(b, a) for a, b in up])
    return jnp.concatenate([low, wide, high], axis=1)


def shards(inputs, w_query, w_key, w_value, w_out, grad_out):
    frames, rows, cols, width = inputs.shape
    tm, height = lax.axis_size("tm"), lax.axis_size("height")
    slots = (2 if tm == 2 else 3) * frames
    dims = (frames, rows, cols, slots, tm, height)
    edge = PAD * cols
    tokens = rows * cols
    wide = tokens + 2 * edge
    x = around(inputs.reshape(frames, tokens, width), edge)
    go = around(grad_out.reshape(frames, tokens, width), edge)
    keys = slots * (BR + 2 * PAD) * cols
    mine = frames * BR * cols
    params = pltpu.CompilerParams(vmem_limit_bytes=56 * 1024 * 1024)
    vmem = pl.BlockSpec(memory_space=pltpu.VMEM)
    attended, dq, stat, k, v = pl.pallas_call(
        functools.partial(first_kernel, dims),
        out_shape=[
            jax.ShapeDtypeStruct((frames, tokens, width), BF),
            jax.ShapeDtypeStruct((frames, tokens, width), BF),
            jax.ShapeDtypeStruct((frames, tokens, 128), F32),
            jax.ShapeDtypeStruct((slots, wide, width), BF),
            jax.ShapeDtypeStruct((slots, wide, width), BF),
        ],
        in_specs=[vmem] * 6,
        out_specs=[vmem] * 5,
        scratch_shapes=[
            pltpu.VMEM((frames, wide, width), BF),
            pltpu.VMEM((frames, wide, width), BF),
            pltpu.VMEM((frames, tokens, width), BF),
            pltpu.VMEM((mine, keys), F32),
        ],
        compiler_params=params,
        name="forward",
    )(x, go, w_query, w_key, w_value, w_out)
    stat = around(stat, edge)
    grad_in = pl.pallas_call(
        functools.partial(second_kernel, dims),
        out_shape=jax.ShapeDtypeStruct((frames, tokens, width), BF),
        in_specs=[vmem] * 10,
        out_specs=vmem,
        scratch_shapes=[
            pltpu.VMEM((slots, wide, width), BF),
            pltpu.VMEM((slots, wide, width), BF),
            pltpu.VMEM((frames, tokens, width), BF),
            pltpu.VMEM((frames, tokens, width), BF),
            pltpu.VMEM((mine, keys), F32),
            pltpu.VMEM((128, keys), F32),
        ],
        compiler_params=params,
        name="backward",
    )(x, go, w_query, w_key, w_value, w_out, k, v, dq, stat)
    shape = (frames, rows, cols, width)
    return attended.reshape(shape), grad_in.reshape(shape)


def solution(mesh):
    placed = (P("tm", "height", None, None), P(), P(), P(), P(), P("tm", "height", None, None))
    return jax.shard_map(
        shards,
        mesh=mesh,
        in_specs=placed,
        out_specs=(P("tm", "height", None, None), P("tm", "height", None, None)),
        check_vma=False,
    )
```

```python
import functools

import jax
import jax.numpy as jnp
from jax import lax
from jax.experimental import pallas as pl
from jax.experimental.pallas import tpu as pltpu
from jax.sharding import PartitionSpec as P

HD = 64
RT = 2
RH = 7
RW = 7
PAD = 8
BR = 8
NHG = 4
BF = jnp.bfloat16
F32 = jnp.float32


def dot_nn(a, b):
    return jnp.dot(a, b, preferred_element_type=F32)


def dot_nt(a, b):
    return lax.dot_general(a, b, (((1,), (1,)), ((), ())), preferred_element_type=F32)


def stack_heads(a):
    head = lax.broadcasted_iota(jnp.int32, a.shape, 1) // HD
    return jnp.concatenate([jnp.where(head == h, a, jnp.zeros_like(a)) for h in range(NHG)], axis=0)


def pick_heads(a):
    n = a.shape[0] // NHG
    head = lax.broadcasted_iota(jnp.int32, (n, a.shape[1]), 1) // HD
    out = a[:n]
    for h in range(1, NHG):
        out = jnp.where(head == h, a[h * n : (h + 1) * n], out)
    return out


def make_bias(block, dims):
    frames, rows, cols, slots, tm_size, height_size = dims
    t = lax.axis_index("tm")
    first = lax.axis_index("height") * rows
    span = (BR + 2 * PAD) * cols
    own = BR * cols
    shape = (frames * own, slots * span)
    i = lax.broadcasted_iota(jnp.int32, shape, 0)
    j = lax.broadcasted_iota(jnp.int32, shape, 1)
    qf = t * frames + i // own
    qr = (i % own) // cols
    slot = j // span
    kr = (j % span) // cols
    group = slot // frames
    if slots == 2 * frames:
        base = jnp.where(group == 0, t, 1 - t)
    else:
        base = jnp.where(group == 0, t, jnp.where(group == 1, t - 1, t + 1))
    kf = base * frames + slot % frames
    near = (jnp.abs(kf - qf) <= RT) & (jnp.abs(kr - PAD - qr) <= RH)
    row = first + block * BR + kr - PAD
    real = (kf >= 0) & (kf < tm_size * frames) & (row >= 0) & (row < height_size * rows)
    return jnp.where(near & real, 0.0, -1e30).astype(F32)


def forward_block(b, g, dims, q_ref, k_ref, v_ref, g_ref, mixed_ref, dq_ref, stat, bias):
    frames, rows, cols, slots, _, _ = dims
    own = BR * cols
    span = (BR + 2 * PAD) * cols
    width = NHG * HD
    at = pl.ds(g * width, width)
    mine = pl.ds(pl.multiple_of((b + 1) * own, own), own)
    inner = pl.ds(pl.multiple_of(b * own, own), own)
    wide = pl.ds(pl.multiple_of(b * own, own), span)
    q = stack_heads(q_ref[:frames, mine, at].reshape(frames * own, width))
    gr = stack_heads(g_ref[:frames, mine, at].reshape(frames * own, width))
    k = k_ref[:, wide, at].reshape(slots * span, width)
    v = v_ref[:, wide, at].reshape(slots * span, width)
    n = frames * own
    s = dot_nt(q, k)
    s = (s.reshape(NHG, n, slots * span) + bias[None]).reshape(NHG * n, slots * span)
    top = jnp.max(s, axis=1, keepdims=True)
    e = jnp.exp(s - top)
    total = jnp.sum(e, axis=1, keepdims=True)
    p = e * (1.0 / total)
    mixed = dot_nn(p.astype(BF), v).astype(BF)
    delta = jnp.sum(gr.astype(F32) * mixed.astype(F32), axis=1, keepdims=True)
    dp = dot_nt(gr, v)
    ds = (p * (dp - delta)).astype(BF)
    dq = dot_nn(ds, k)
    mixed_ref[:, inner, at] = pick_heads(mixed).reshape(frames, own, width)
    dq = pick_heads(dq) * HD ** (-0.5)
    dq_ref[:, inner, at] = dq.astype(BF).reshape(frames, own, width)
    lse = top + jnp.log(total)
    lane = lax.broadcasted_iota(jnp.int32, (n, 128), 1)
    for h in range(NHG):
        stat = jnp.where(lane == g * NHG + h, lse[h * n : (h + 1) * n], stat)
        stat = jnp.where(lane == 64 + g * NHG + h, delta[h * n : (h + 1) * n], stat)
    return stat


def backward_block(b, g, dims, q_ref, k_ref, v_ref, g_ref, dk_ref, dv_ref, flip, bias):
    frames, rows, cols, slots, _, _ = dims
    own = BR * cols
    span = (BR + 2 * PAD) * cols
    width = NHG * HD
    at = pl.ds(g * width, width)
    mine = pl.ds(pl.multiple_of((b + 1) * own, own), own)
    inner = pl.ds(pl.multiple_of(b * own, own), own)
    wide = pl.ds(pl.multiple_of(b * own, own), span)
    k = stack_heads(k_ref[:frames, mine, at].reshape(frames * own, width))
    v = stack_heads(v_ref[:frames, mine, at].reshape(frames * own, width))
    q = q_ref[:, wide, at].reshape(slots * span, width)
    gr = g_ref[:, wide, at].reshape(slots * span, width)
    n = frames * own
    full = (NHG, n, slots * span)
    lse = flip[g * NHG : (g + 1) * NHG, :]
    delta = flip[64 + g * NHG : 64 + (g + 1) * NHG, :]
    s = dot_nt(k, q).reshape(full)
    p = jnp.exp(s + bias[None] - lse[:, None, :])
    dv = dot_nn(p.astype(BF).reshape(NHG * n, -1), gr)
    dp = dot_nt(v, gr).reshape(full)
    ds = (p * (dp - delta[:, None, :])).astype(BF)
    dk = dot_nn(ds.reshape(NHG * n, -1), q)
    dk_ref[:, inner, at] = pick_heads(dk).astype(BF).reshape(frames, own, width)
    dv_ref[:, inner, at] = pick_heads(dv).astype(BF).reshape(frames, own, width)


def project(src_ref, jobs, slots, spans):
    width = src_ref.shape[2]
    tile = 256
    first, count = slots
    some = pl.ds(first, count)
    total = sum(size for _, size in spans)

    def step(i, _):
        at = pl.ds(pl.multiple_of(i * tile, tile), tile)
        parts = [src_ref[some, a : a + size, :].reshape(count * size, width) for a, size in spans]
        rows = parts[0] if len(parts) == 1 else jnp.concatenate(parts, axis=0)
        for w_ref, dst_ref, flip, factor in jobs:
            out = dot_nt(rows, w_ref[at, :]) if flip else dot_nn(rows, w_ref[:, at])
            out = out.astype(BF)
            if factor != 1:
                out = out * jnp.asarray(factor, BF)
            begin = 0
            for a, size in spans:
                piece = out[begin : begin + count * size]
                dst_ref[some, a : a + size, at] = piece.reshape(count, size, tile)
                begin += count * size
        return 0

    lax.fori_loop(0, width // tile, step, 0)


class Exchange:
    def __init__(self, ref, sems, dims, edge):
        frames, rows, cols, slots, tm, height = dims
        self.ref, self.edge, self.frames = ref, edge, frames
        self.t, self.h = lax.axis_index("tm"), lax.axis_index("height")
        self.tm, self.height = tm, height
        self.send_x, self.recv_x, self.send_h, self.recv_h = sems
        tokens = rows * cols
        self.pieces = [(edge, edge), (tokens, edge), (2 * edge, tokens - 2 * edge)]
        self.groups = slots // frames

    def links(self):
        if self.tm == 2:
            return [(1, 1 - self.t, None, None)]
        return [
            (1, self.t + 1, self.t < self.tm - 1, self.t > 0),
            (2, self.t - 1, self.t > 0, self.t < self.tm - 1),
        ]

    def tm_copy(self, link, piece):
        group, target, _, _ = self.links()[link]
        start, size = self.pieces[piece]
        rows = pl.ds(start, size)
        return pltpu.make_async_remote_copy(
            src_ref=self.ref.at[pl.ds(0, self.frames), rows],
            dst_ref=self.ref.at[pl.ds(group * self.frames, self.frames), rows],
            send_sem=self.send_x.at[link * 3 + piece],
            recv_sem=self.recv_x.at[link * 3 + piece],
            device_id=(target, self.h),
            device_id_type=pl.DeviceIdType.MESH,
        )

    def row_copy(self, group, up):
        low, high = self.pieces[0][0], self.pieces[1][0]
        end = high + self.edge
        some = pl.ds(group * self.frames, self.frames)
        src, dst = (high, 0) if up else (low, end)
        slot = group * 2 + int(up)
        return pltpu.make_async_remote_copy(
            src_ref=self.ref.at[some, pl.ds(src, self.edge)],
            dst_ref=self.ref.at[some, pl.ds(dst, self.edge)],
            send_sem=self.send_h.at[slot],
            recv_sem=self.recv_h.at[slot],
            device_id=(self.t, self.h + 1 if up else self.h - 1),
            device_id_type=pl.DeviceIdType.MESH,
        )

    def when(self, cond, act):
        if cond is None:
            act()
        else:
            pl.when(cond)(act)

    def clear(self):
        low, end = self.edge, self.pieces[1][0] + self.edge
        shape = self.ref.shape

        @pl.when(self.h == 0)
        def _():
            self.ref[:, 0:low, :] = jnp.zeros((shape[0], low, shape[2]), self.ref.dtype)

        @pl.when(self.h == self.height - 1)
        def _():
            self.ref[:, end:, :] = jnp.zeros((shape[0], low, shape[2]), self.ref.dtype)

        for group, _, _, there in self.links():
            if there is not None:

                @pl.when(jnp.logical_not(there))
                def _(group=group):
                    some = pl.ds(group * self.frames, self.frames)
                    self.ref[some, low:end, :] = jnp.zeros((self.frames, end - low, shape[2]), self.ref.dtype)

    def there(self, group):
        return None if group == 0 else self.links()[group - 1][3]

    def both(self, a, b):
        return b if a is None else a & b

    def send_tm(self):
        for piece in range(3):
            for link, (_, _, sends, _) in enumerate(self.links()):
                self.when(sends, lambda link=link, piece=piece: self.tm_copy(link, piece).start())

    def got_tm(self, pieces):
        for link, (_, _, _, gets) in enumerate(self.links()):
            for piece in pieces:
                self.when(gets, lambda link=link, piece=piece: self.tm_copy(link, piece).wait_recv())

    def send_rows(self, groups):
        for group in groups:
            there = self.there(group)
            self.when(self.both(there, self.h < self.height - 1), lambda g=group: self.row_copy(g, True).start())
            self.when(self.both(there, self.h > 0), lambda g=group: self.row_copy(g, False).start())

    def got_rows(self):
        for group in range(self.groups):
            there = self.there(group)
            self.when(self.both(there, self.h > 0), lambda g=group: self.row_copy(g, True).wait_recv())
            self.when(self.both(there, self.h < self.height - 1), lambda g=group: self.row_copy(g, False).wait_recv())

    def sent(self):
        for piece in range(3):
            for link, (_, _, sends, _) in enumerate(self.links()):
                self.when(sends, lambda link=link, piece=piece: self.tm_copy(link, piece).wait_send())
        for group in range(self.groups):
            there = self.there(group)
            self.when(self.both(there, self.h < self.height - 1), lambda g=group: self.row_copy(g, True).wait_send())
            self.when(self.both(there, self.h > 0), lambda g=group: self.row_copy(g, False).wait_send())


def meet(dims):
    _, _, _, _, tm, height = dims
    t, h = lax.axis_index("tm"), lax.axis_index("height")
    barrier = pltpu.get_barrier_semaphore()
    count = jnp.int32(0)
    others = [(h > 0, t, h - 1), (h < height - 1, t, h + 1)]
    if tm == 2:
        pl.semaphore_signal(barrier, inc=1, device_id=(1 - t, h), device_id_type=pl.DeviceIdType.MESH)
        count = count + 1
    else:
        others += [(t > 0, t - 1, h), (t < tm - 1, t + 1, h)]
    for cond, tt, hh in others:

        @pl.when(cond)
        def _(tt=tt, hh=hh):
            pl.semaphore_signal(barrier, inc=1, device_id=(tt, hh), device_id_type=pl.DeviceIdType.MESH)

        count = count + cond.astype(jnp.int32)
    pl.semaphore_wait(barrier, count)


def kernel(
    dims, x_hbm, go_hbm, wq_hbm, wk_hbm, wv_hbm, wo_hbm,
    attended_ref, out_ref,
    x_ref, go_ref, q_ref, k_ref, v_ref, g_ref, wq_ref, wk_ref, wv_ref, wo_ref,
    mixed_ref, dq_ref, dk_ref, dv_ref, stat_ref, bias_ref, local_sem,
    *sems,
):
    frames, rows, cols, slots, tm, height = dims
    width = x_ref.shape[2]
    own = BR * cols
    span = (BR + 2 * PAD) * cols
    edge = PAD * cols
    tokens = rows * cols
    blocks = rows // BR
    scale = HD ** (-0.5)
    mid = pl.ds(edge, tokens)
    loads = [
        pltpu.make_async_copy(x_hbm, x_ref.at[pl.ds(0, frames), mid], local_sem.at[0]),
        pltpu.make_async_copy(go_hbm, go_ref.at[pl.ds(0, frames), mid], local_sem.at[1]),
        pltpu.make_async_copy(wq_hbm, wq_ref, local_sem.at[2]),
        pltpu.make_async_copy(wk_hbm, wk_ref, local_sem.at[3]),
        pltpu.make_async_copy(wv_hbm, wv_ref, local_sem.at[4]),
        pltpu.make_async_copy(wo_hbm, wo_ref, local_sem.at[5]),
    ]
    for load in loads:
        load.start()
    ex_x = Exchange(x_ref, sems[0:4], dims, edge)
    ex_go = Exchange(go_ref, sems[4:8], dims, edge)
    ex_st = Exchange(stat_ref, sems[8:12], dims, edge)
    meet(dims)
    loads[0].wait()
    ex_x.send_tm()
    ex_x.send_rows([0])
    loads[1].wait()
    ex_go.send_tm()
    ex_go.send_rows([0])
    ex_x.clear()
    ex_go.clear()
    ex_st.clear()

    def fill(b, _):
        bias_ref[b] = make_bias(b, dims)
        return 0

    lax.fori_loop(0, blocks, fill, 0)
    centre = [(edge, tokens)]
    rims = [(0, edge), (edge + tokens, edge)]
    for load in loads[2:5]:
        load.wait()
    to_q = (wq_ref, q_ref, False, scale)
    to_k = (wk_ref, k_ref, False, 1)
    to_v = (wv_ref, v_ref, False, 1)
    to_g = (wo_ref, g_ref, True, 1)
    project(x_ref, [to_q, to_k, to_v], (0, frames), centre)
    loads[5].wait()
    project(go_ref, [to_g], (0, frames), centre)

    def forward(b):
        stat = jnp.zeros((frames * own, 128), F32)
        bias = bias_ref[b]
        for g in range(width // (NHG * HD)):
            stat = forward_block(b, g, dims, q_ref, k_ref, v_ref, g_ref, mixed_ref, dq_ref, stat, bias)
        at = pl.ds(pl.multiple_of((b + 1) * own, own), own)
        stat_ref[pl.ds(0, frames), at, :] = stat.reshape(frames, own, 128)

    def backward(b):
        at = pl.ds(pl.multiple_of(b * own, own), span)
        flip = stat_ref[:, at, :].reshape(slots * span, 128).T
        bias = bias_ref[b]
        for g in range(width // (NHG * HD)):
            backward_block(b, g, dims, q_ref, k_ref, v_ref, g_ref, dk_ref, dv_ref, flip, bias)

    def inner_blocks(act):
        def step(b, _):
            act(b)
            return 0

        lax.fori_loop(1, blocks - 1, step, 0)

    def outer_blocks(act):
        def step(i, _):
            act(i * (blocks - 1))
            return 0

        lax.fori_loop(0, 2, step, 0)

    others = list(range(1, slots // frames))
    ex_x.got_tm([0, 1])
    ex_x.send_rows(others)
    ex_x.got_tm([2])
    project(x_ref, [to_k, to_v], (frames, slots - frames), centre)
    inner_blocks(forward)
    ex_go.got_tm([0, 1])
    ex_go.send_rows(others)
    ex_x.got_rows()
    project(x_ref, [to_k, to_v], (0, slots), rims)
    outer_blocks(forward)
    ex_st.send_tm()
    ex_st.send_rows([0])
    project(mixed_ref, [(wo_ref, attended_ref, False, 1)], (0, frames), [(0, tokens)])
    ex_go.got_tm([2])
    ex_st.got_tm([0, 1])
    ex_st.send_rows(others)
    project(x_ref, [to_q], (frames, slots - frames), centre)
    project(go_ref, [to_g], (frames, slots - frames), centre)
    ex_st.got_tm([2])
    inner_blocks(backward)
    ex_go.got_rows()
    project(x_ref, [to_q], (0, slots), rims)
    project(go_ref, [to_g], (0, slots), rims)
    ex_st.got_rows()
    outer_blocks(backward)
    tile = 256

    def out_step(i, _):
        at = pl.ds(pl.multiple_of(i * tile, tile), tile)
        total = dot_nt(dq_ref[...].reshape(frames * tokens, width), wq_ref[at, :])
        total += dot_nt(dk_ref[...].reshape(frames * tokens, width), wk_ref[at, :])
        total += dot_nt(dv_ref[...].reshape(frames * tokens, width), wv_ref[at, :])
        out_ref[:, :, at] = total.astype(BF).reshape(frames, tokens, tile)
        return 0

    lax.fori_loop(0, width // tile, out_step, 0)
    ex_x.sent()
    ex_go.sent()
    ex_st.sent()


def shards(inputs, w_query, w_key, w_value, w_out, grad_out):
    frames, rows, cols, width = inputs.shape
    tm, height = lax.axis_size("tm"), lax.axis_size("height")
    groups = 2 if tm == 2 else 3
    slots = groups * frames
    dims = (frames, rows, cols, slots, tm, height)
    tokens = rows * cols
    wide = tokens + 2 * PAD * cols
    keys = slots * (BR + 2 * PAD) * cols
    mine = frames * BR * cols
    vmem = pl.BlockSpec(memory_space=pltpu.VMEM)
    hbm = pl.BlockSpec(memory_space=pl.ANY)
    links = 3 * (groups - 1)
    sems = [pltpu.SemaphoreType.DMA((links,))] * 2 + [pltpu.SemaphoreType.DMA((2 * groups,))] * 2
    attended, grad_in = pl.pallas_call(
        functools.partial(kernel, dims),
        out_shape=[jax.ShapeDtypeStruct((frames, tokens, width), BF)] * 2,
        in_specs=[hbm] * 6,
        out_specs=[vmem] * 2,
        scratch_shapes=[pltpu.VMEM((slots, wide, width), BF)] * 6
        + [pltpu.VMEM((width, width), BF)] * 4
        + [pltpu.VMEM((frames, tokens, width), BF)] * 4
        + [
            pltpu.VMEM((slots, wide, 128), F32),
            pltpu.VMEM((rows // BR, mine, keys), F32),
            pltpu.SemaphoreType.DMA((6,)),
        ]
        + sems * 3,
        compiler_params=pltpu.CompilerParams(
            vmem_limit_bytes=56 * 1024 * 1024, collective_id=0, has_side_effects=True
        ),
        name="attention",
    )(
        inputs.reshape(frames, tokens, width), grad_out.reshape(frames, tokens, width),
        w_query, w_key, w_value, w_out,
    )
    shape = (frames, rows, cols, width)
    return attended.reshape(shape), grad_in.reshape(shape)


def solution(mesh):
    placed = (P("tm", "height", None, None), P(), P(), P(), P(), P("tm", "height", None, None))
    return jax.shard_map(
        shards,
        mesh=mesh,
        in_specs=placed,
        out_specs=(P("tm", "height", None, None), P("tm", "height", None, None)),
        check_vma=False,
    )
```

```python
import functools

import jax
import jax.numpy as jnp
from jax import lax
from jax.experimental import pallas as pl
from jax.experimental.pallas import tpu as pltpu
from jax.sharding import PartitionSpec as P

HD = 64
RT = 2
RH = 7
RW = 7
PAD = 8
BR = 8
NHG = 4
BF = jnp.bfloat16
F32 = jnp.float32


def dot_nn(a, b):
    return jnp.dot(a, b, preferred_element_type=F32)


def dot_nt(a, b):
    return lax.dot_general(a, b, (((1,), (1,)), ((), ())), preferred_element_type=F32)


def stack_heads(a):
    head = lax.broadcasted_iota(jnp.int32, a.shape, 1) // HD
    return jnp.concatenate([jnp.where(head == h, a, jnp.zeros_like(a)) for h in range(NHG)], axis=0)


def pick_heads(a):
    n = a.shape[0] // NHG
    head = lax.broadcasted_iota(jnp.int32, (n, a.shape[1]), 1) // HD
    out = a[:n]
    for h in range(1, NHG):
        out = jnp.where(head == h, a[h * n : (h + 1) * n], out)
    return out


def make_bias(block, dims):
    frames, rows, cols, slots, tm_size, height_size = dims
    t = lax.axis_index("tm")
    first = lax.axis_index("height") * rows
    span = (BR + 2 * PAD) * cols
    own = BR * cols
    shape = (frames * own, slots * span)
    i = lax.broadcasted_iota(jnp.int32, shape, 0)
    j = lax.broadcasted_iota(jnp.int32, shape, 1)
    qf = t * frames + i // own
    qr = (i % own) // cols
    slot = j // span
    kr = (j % span) // cols
    group = slot // frames
    if slots == 2 * frames:
        base = jnp.where(group == 0, t, 1 - t)
    else:
        base = jnp.where(group == 0, t, jnp.where(group == 1, t - 1, t + 1))
    kf = base * frames + slot % frames
    near = (jnp.abs(kf - qf) <= RT) & (jnp.abs(kr - PAD - qr) <= RH)
    row = first + block * BR + kr - PAD
    real = (kf >= 0) & (kf < tm_size * frames) & (row >= 0) & (row < height_size * rows)
    return jnp.where(near & real, 0.0, -1e30).astype(F32)


def forward_block(b, g, dims, q_ref, k_ref, v_ref, g_ref, mixed_ref, dq_ref, stat, bias):
    frames, rows, cols, slots, _, _ = dims
    own = BR * cols
    span = (BR + 2 * PAD) * cols
    width = NHG * HD
    at = pl.ds(g * width, width)
    mine = pl.ds(pl.multiple_of((b + 1) * own, own), own)
    inner = pl.ds(pl.multiple_of(b * own, own), own)
    wide = pl.ds(pl.multiple_of(b * own, own), span)
    q = stack_heads(q_ref[:frames, mine, at].reshape(frames * own, width))
    gr = stack_heads(g_ref[:frames, mine, at].reshape(frames * own, width))
    k = k_ref[:, wide, at].reshape(slots * span, width)
    v = v_ref[:, wide, at].reshape(slots * span, width)
    n = frames * own
    s = dot_nt(q, k)
    s = (s.reshape(NHG, n, slots * span) + bias[None]).reshape(NHG * n, slots * span)
    top = jnp.max(s, axis=1, keepdims=True)
    e = jnp.exp(s - top)
    total = jnp.sum(e, axis=1, keepdims=True)
    p = e * (1.0 / total)
    mixed = dot_nn(p.astype(BF), v).astype(BF)
    delta = jnp.sum(gr.astype(F32) * mixed.astype(F32), axis=1, keepdims=True)
    dp = dot_nt(gr, v)
    ds = (p * (dp - delta)).astype(BF)
    dq = dot_nn(ds, k)
    mixed_ref[:, inner, at] = pick_heads(mixed).reshape(frames, own, width)
    dq = pick_heads(dq) * HD ** (-0.5)
    dq_ref[:, inner, at] = dq.astype(BF).reshape(frames, own, width)
    lse = top + jnp.log(total)
    lane = lax.broadcasted_iota(jnp.int32, (n, 128), 1)
    for h in range(NHG):
        stat = jnp.where(lane == g * NHG + h, lse[h * n : (h + 1) * n], stat)
        stat = jnp.where(lane == 64 + g * NHG + h, delta[h * n : (h + 1) * n], stat)
    return stat


def backward_block(b, g, dims, q_ref, k_ref, v_ref, g_ref, dk_ref, dv_ref, flip, bias):
    frames, rows, cols, slots, _, _ = dims
    own = BR * cols
    span = (BR + 2 * PAD) * cols
    width = NHG * HD
    at = pl.ds(g * width, width)
    mine = pl.ds(pl.multiple_of((b + 1) * own, own), own)
    inner = pl.ds(pl.multiple_of(b * own, own), own)
    wide = pl.ds(pl.multiple_of(b * own, own), span)
    k = stack_heads(k_ref[:frames, mine, at].reshape(frames * own, width))
    v = stack_heads(v_ref[:frames, mine, at].reshape(frames * own, width))
    q = q_ref[:, wide, at].reshape(slots * span, width)
    gr = g_ref[:, wide, at].reshape(slots * span, width)
    n = frames * own
    full = (NHG, n, slots * span)
    lse = flip[g * NHG : (g + 1) * NHG, :]
    delta = flip[64 + g * NHG : 64 + (g + 1) * NHG, :]
    s = dot_nt(k, q).reshape(full)
    p = jnp.exp(s + bias[None] - lse[:, None, :])
    dv = dot_nn(p.astype(BF).reshape(NHG * n, -1), gr)
    dp = dot_nt(v, gr).reshape(full)
    ds = (p * (dp - delta[:, None, :])).astype(BF)
    dk = dot_nn(ds.reshape(NHG * n, -1), q)
    dk_ref[:, inner, at] = pick_heads(dk).astype(BF).reshape(frames, own, width)
    dv_ref[:, inner, at] = pick_heads(dv).astype(BF).reshape(frames, own, width)


def project(src_ref, jobs, slots, spans):
    width = src_ref.shape[2]
    tile = 256
    first, count = slots
    some = pl.ds(first, count)
    total = sum(size for _, size in spans)

    def step(i, _):
        at = pl.ds(pl.multiple_of(i * tile, tile), tile)
        parts = [src_ref[some, a : a + size, :].reshape(count * size, width) for a, size in spans]
        rows = parts[0] if len(parts) == 1 else jnp.concatenate(parts, axis=0)
        for w_ref, dst_ref, flip, factor in jobs:
            out = dot_nt(rows, w_ref[at, :]) if flip else dot_nn(rows, w_ref[:, at])
            out = out.astype(BF)
            if factor != 1:
                out = out * jnp.asarray(factor, BF)
            begin = 0
            for a, size in spans:
                piece = out[begin : begin + count * size]
                if len(dst_ref.shape) == 4:
                    dst_ref[some, :, :, at] = piece.reshape(count, *dst_ref.shape[1:3], tile)
                else:
                    dst_ref[some, a : a + size, at] = piece.reshape(count, size, tile)
                begin += count * size
        return 0

    lax.fori_loop(0, width // tile, step, 0)


class Exchange:
    def __init__(self, ref, sems, dims, edge):
        frames, rows, cols, slots, tm, height = dims
        self.ref, self.edge, self.frames = ref, edge, frames
        self.t, self.h = lax.axis_index("tm"), lax.axis_index("height")
        self.tm, self.height = tm, height
        self.send_x, self.recv_x, self.send_h, self.recv_h = sems
        tokens = rows * cols
        self.pieces = [(edge, edge), (tokens, edge), (2 * edge, tokens - 2 * edge)]
        self.groups = slots // frames

    def links(self):
        if self.tm == 2:
            return [(1, 1 - self.t, None, None)]
        return [
            (1, self.t + 1, self.t < self.tm - 1, self.t > 0),
            (2, self.t - 1, self.t > 0, self.t < self.tm - 1),
        ]

    def tm_copy(self, link, piece):
        group, target, _, _ = self.links()[link]
        start, size = self.pieces[piece]
        rows = pl.ds(start, size)
        return pltpu.make_async_remote_copy(
            src_ref=self.ref.at[pl.ds(0, self.frames), rows],
            dst_ref=self.ref.at[pl.ds(group * self.frames, self.frames), rows],
            send_sem=self.send_x.at[link * 3 + piece],
            recv_sem=self.recv_x.at[link * 3 + piece],
            device_id=(target, self.h),
            device_id_type=pl.DeviceIdType.MESH,
        )

    def row_copy(self, group, up):
        low, high = self.pieces[0][0], self.pieces[1][0]
        end = high + self.edge
        some = pl.ds(group * self.frames, self.frames)
        src, dst = (high, 0) if up else (low, end)
        slot = group * 2 + int(up)
        return pltpu.make_async_remote_copy(
            src_ref=self.ref.at[some, pl.ds(src, self.edge)],
            dst_ref=self.ref.at[some, pl.ds(dst, self.edge)],
            send_sem=self.send_h.at[slot],
            recv_sem=self.recv_h.at[slot],
            device_id=(self.t, self.h + 1 if up else self.h - 1),
            device_id_type=pl.DeviceIdType.MESH,
        )

    def when(self, cond, act):
        if cond is None:
            act()
        else:
            pl.when(cond)(act)

    def clear(self):
        low, end = self.edge, self.pieces[1][0] + self.edge
        shape = self.ref.shape

        @pl.when(self.h == 0)
        def _():
            self.ref[:, 0:low, :] = jnp.zeros((shape[0], low, shape[2]), self.ref.dtype)

        @pl.when(self.h == self.height - 1)
        def _():
            self.ref[:, end:, :] = jnp.zeros((shape[0], low, shape[2]), self.ref.dtype)

        for group, _, _, there in self.links():
            if there is not None:

                @pl.when(jnp.logical_not(there))
                def _(group=group):
                    some = pl.ds(group * self.frames, self.frames)
                    self.ref[some, low:end, :] = jnp.zeros((self.frames, end - low, shape[2]), self.ref.dtype)

    def there(self, group):
        return None if group == 0 else self.links()[group - 1][3]

    def both(self, a, b):
        return b if a is None else a & b

    def send_tm(self):
        for piece in range(3):
            for link, (_, _, sends, _) in enumerate(self.links()):
                self.when(sends, lambda link=link, piece=piece: self.tm_copy(link, piece).start())

    def got_tm(self, pieces):
        for link, (_, _, _, gets) in enumerate(self.links()):
            for piece in pieces:
                self.when(gets, lambda link=link, piece=piece: self.tm_copy(link, piece).wait_recv())

    def send_rows(self, groups):
        for group in groups:
            there = self.there(group)
            self.when(self.both(there, self.h < self.height - 1), lambda g=group: self.row_copy(g, True).start())
            self.when(self.both(there, self.h > 0), lambda g=group: self.row_copy(g, False).start())

    def got_rows(self):
        for group in range(self.groups):
            there = self.there(group)
            self.when(self.both(there, self.h > 0), lambda g=group: self.row_copy(g, True).wait_recv())
            self.when(self.both(there, self.h < self.height - 1), lambda g=group: self.row_copy(g, False).wait_recv())

    def sent(self):
        for piece in range(3):
            for link, (_, _, sends, _) in enumerate(self.links()):
                self.when(sends, lambda link=link, piece=piece: self.tm_copy(link, piece).wait_send())
        for group in range(self.groups):
            there = self.there(group)
            self.when(self.both(there, self.h < self.height - 1), lambda g=group: self.row_copy(g, True).wait_send())
            self.when(self.both(there, self.h > 0), lambda g=group: self.row_copy(g, False).wait_send())


def meet(dims):
    _, _, _, _, tm, height = dims
    t, h = lax.axis_index("tm"), lax.axis_index("height")
    barrier = pltpu.get_barrier_semaphore()
    count = jnp.int32(0)
    others = [(h > 0, t, h - 1), (h < height - 1, t, h + 1)]
    if tm == 2:
        pl.semaphore_signal(barrier, inc=1, device_id=(1 - t, h), device_id_type=pl.DeviceIdType.MESH)
        count = count + 1
    else:
        others += [(t > 0, t - 1, h), (t < tm - 1, t + 1, h)]
    for cond, tt, hh in others:

        @pl.when(cond)
        def _(tt=tt, hh=hh):
            pl.semaphore_signal(barrier, inc=1, device_id=(tt, hh), device_id_type=pl.DeviceIdType.MESH)

        count = count + cond.astype(jnp.int32)
    pl.semaphore_wait(barrier, count)


def kernel(
    dims, x_hbm, go_hbm, wq_hbm, wk_hbm, wv_hbm, wo_hbm,
    attended_ref, out_ref,
    x_ref, go_ref, q_ref, k_ref, v_ref, g_ref, wq_ref, wk_ref, wv_ref, wo_ref,
    mixed_ref, dq_ref, dk_ref, dv_ref, stat_ref, bias_ref, x4_ref, go4_ref, local_sem,
    *sems,
):
    frames, rows, cols, slots, tm, height = dims
    width = x_ref.shape[2]
    own = BR * cols
    span = (BR + 2 * PAD) * cols
    edge = PAD * cols
    tokens = rows * cols
    blocks = rows // BR
    scale = HD ** (-0.5)
    mid = pl.ds(edge, tokens)
    loads = [
        pltpu.make_async_copy(x_hbm, x4_ref, local_sem.at[0]),
        pltpu.make_async_copy(go_hbm, go4_ref, local_sem.at[1]),
        pltpu.make_async_copy(wq_hbm, wq_ref, local_sem.at[2]),
        pltpu.make_async_copy(wk_hbm, wk_ref, local_sem.at[3]),
        pltpu.make_async_copy(wv_hbm, wv_ref, local_sem.at[4]),
        pltpu.make_async_copy(wo_hbm, wo_ref, local_sem.at[5]),
    ]
    for load in loads:
        load.start()
    ex_x = Exchange(x_ref, sems[0:4], dims, edge)
    ex_go = Exchange(go_ref, sems[4:8], dims, edge)
    ex_st = Exchange(stat_ref, sems[8:12], dims, edge)
    loads[0].wait()
    x_ref[pl.ds(0, frames), mid, :] = x4_ref[...].reshape(frames, tokens, width)
    meet(dims)
    ex_x.send_tm()
    ex_x.send_rows([0])
    loads[1].wait()
    go_ref[pl.ds(0, frames), mid, :] = go4_ref[...].reshape(frames, tokens, width)
    ex_go.send_tm()
    ex_go.send_rows([0])
    ex_x.clear()
    ex_go.clear()
    ex_st.clear()

    def fill(b, _):
        bias_ref[b] = make_bias(b, dims)
        return 0

    lax.fori_loop(0, blocks, fill, 0)
    centre = [(edge, tokens)]
    rims = [(0, edge), (edge + tokens, edge)]
    for load in loads[2:5]:
        load.wait()
    to_q = (wq_ref, q_ref, False, scale)
    to_k = (wk_ref, k_ref, False, 1)
    to_v = (wv_ref, v_ref, False, 1)
    to_g = (wo_ref, g_ref, True, 1)
    project(x_ref, [to_q, to_k, to_v], (0, frames), centre)
    loads[5].wait()
    project(go_ref, [to_g], (0, frames), centre)

    def forward(b):
        stat = jnp.zeros((frames * own, 128), F32)
        bias = bias_ref[b]
        for g in range(width // (NHG * HD)):
            stat = forward_block(b, g, dims, q_ref, k_ref, v_ref, g_ref, mixed_ref, dq_ref, stat, bias)
        at = pl.ds(pl.multiple_of((b + 1) * own, own), own)
        stat_ref[pl.ds(0, frames), at, :] = stat.reshape(frames, own, 128)

    def backward(b):
        at = pl.ds(pl.multiple_of(b * own, own), span)
        flip = stat_ref[:, at, :].reshape(slots * span, 128).T
        bias = bias_ref[b]
        for g in range(width // (NHG * HD)):
            backward_block(b, g, dims, q_ref, k_ref, v_ref, g_ref, dk_ref, dv_ref, flip, bias)

    def inner_blocks(act):
        def step(b, _):
            act(b)
            return 0

        lax.fori_loop(1, blocks - 1, step, 0)

    def outer_blocks(act):
        def step(i, _):
            act(i * (blocks - 1))
            return 0

        lax.fori_loop(0, 2, step, 0)

    others = list(range(1, slots // frames))
    ex_x.got_tm([0, 1])
    ex_x.send_rows(others)
    ex_x.got_tm([2])
    project(x_ref, [to_k, to_v], (frames, slots - frames), centre)
    inner_blocks(forward)
    ex_go.got_tm([0, 1])
    ex_go.send_rows(others)
    ex_x.got_rows()
    project(x_ref, [to_k, to_v], (0, slots), rims)
    outer_blocks(forward)
    ex_st.send_tm()
    ex_st.send_rows([0])
    project(mixed_ref, [(wo_ref, attended_ref, False, 1)], (0, frames), [(0, tokens)])
    ex_go.got_tm([2])
    ex_st.got_tm([0, 1])
    ex_st.send_rows(others)
    project(x_ref, [to_q], (frames, slots - frames), centre)
    project(go_ref, [to_g], (frames, slots - frames), centre)
    ex_st.got_tm([2])
    inner_blocks(backward)
    ex_go.got_rows()
    project(x_ref, [to_q], (0, slots), rims)
    project(go_ref, [to_g], (0, slots), rims)
    ex_st.got_rows()
    outer_blocks(backward)
    tile = 256

    def out_step(i, _):
        at = pl.ds(pl.multiple_of(i * tile, tile), tile)
        total = dot_nt(dq_ref[...].reshape(frames * tokens, width), wq_ref[at, :])
        total += dot_nt(dk_ref[...].reshape(frames * tokens, width), wk_ref[at, :])
        total += dot_nt(dv_ref[...].reshape(frames * tokens, width), wv_ref[at, :])
        out_ref[:, :, :, at] = total.astype(BF).reshape(frames, rows, cols, tile)
        return 0

    lax.fori_loop(0, width // tile, out_step, 0)
    ex_x.sent()
    ex_go.sent()
    ex_st.sent()


def shards(inputs, w_query, w_key, w_value, w_out, grad_out):
    frames, rows, cols, width = inputs.shape
    tm, height = lax.axis_size("tm"), lax.axis_size("height")
    groups = 2 if tm == 2 else 3
    slots = groups * frames
    dims = (frames, rows, cols, slots, tm, height)
    tokens = rows * cols
    wide = tokens + 2 * PAD * cols
    keys = slots * (BR + 2 * PAD) * cols
    mine = frames * BR * cols
    vmem = pl.BlockSpec(memory_space=pltpu.VMEM)
    hbm = pl.BlockSpec(memory_space=pl.ANY)
    links = 3 * (groups - 1)
    sems = [pltpu.SemaphoreType.DMA((links,))] * 2 + [pltpu.SemaphoreType.DMA((2 * groups,))] * 2
    return pl.pallas_call(
        functools.partial(kernel, dims),
        out_shape=[jax.ShapeDtypeStruct(inputs.shape, BF)] * 2,
        in_specs=[hbm] * 6,
        out_specs=[vmem] * 2,
        scratch_shapes=[pltpu.VMEM((slots, wide, width), BF)] * 6
        + [pltpu.VMEM((width, width), BF)] * 4
        + [pltpu.VMEM((frames, tokens, width), BF)] * 4
        + [
            pltpu.VMEM((slots, wide, 128), F32),
            pltpu.VMEM((rows // BR, mine, keys), F32),
            pltpu.VMEM(inputs.shape, BF),
            pltpu.VMEM(inputs.shape, BF),
            pltpu.SemaphoreType.DMA((6,)),
        ]
        + sems * 3,
        compiler_params=pltpu.CompilerParams(
            vmem_limit_bytes=56 * 1024 * 1024, collective_id=0, has_side_effects=True
        ),
        name="attention",
    )(inputs, grad_out, w_query, w_key, w_value, w_out)


def solution(mesh):
    placed = (P("tm", "height", None, None), P(), P(), P(), P(), P("tm", "height", None, None))
    return jax.shard_map(
        shards,
        mesh=mesh,
        in_specs=placed,
        out_specs=(P("tm", "height", None, None), P("tm", "height", None, None)),
        check_vma=False,
    )
```

```python
import functools

import jax
import jax.numpy as jnp
from jax import lax
from jax.experimental import pallas as pl
from jax.experimental.pallas import tpu as pltpu
from jax.sharding import PartitionSpec as P

HD = 64
RT = 2
RH = 7
RW = 7
PAD = 8
BR = 8
NHG = 4
BF = jnp.bfloat16
F32 = jnp.float32


def dot_nn(a, b):
    return jnp.dot(a, b, preferred_element_type=F32)


def dot_nt(a, b):
    return lax.dot_general(a, b, (((1,), (1,)), ((), ())), preferred_element_type=F32)


def stack_heads(a):
    head = lax.broadcasted_iota(jnp.int32, a.shape, 1) // HD
    return jnp.concatenate([jnp.where(head == h, a, jnp.zeros_like(a)) for h in range(NHG)], axis=0)


def pick_heads(a):
    n = a.shape[0] // NHG
    head = lax.broadcasted_iota(jnp.int32, (n, a.shape[1]), 1) // HD
    out = a[:n]
    for h in range(1, NHG):
        out = jnp.where(head == h, a[h * n : (h + 1) * n], out)
    return out


def make_bias(block, dims):
    frames, rows, cols, slots, tm_size, height_size = dims
    t = lax.axis_index("tm")
    first = lax.axis_index("height") * rows
    span = (BR + 2 * PAD) * cols
    own = BR * cols
    shape = (frames * own, slots * span)
    i = lax.broadcasted_iota(jnp.int32, shape, 0)
    j = lax.broadcasted_iota(jnp.int32, shape, 1)
    qf = t * frames + i // own
    qr = (i % own) // cols
    slot = j // span
    kr = (j % span) // cols
    group = slot // frames
    if slots == 2 * frames:
        base = jnp.where(group == 0, t, 1 - t)
    else:
        base = jnp.where(group == 0, t, jnp.where(group == 1, t - 1, t + 1))
    kf = base * frames + slot % frames
    near = (jnp.abs(kf - qf) <= RT) & (jnp.abs(kr - PAD - qr) <= RH)
    row = first + block * BR + kr - PAD
    real = (kf >= 0) & (kf < tm_size * frames) & (row >= 0) & (row < height_size * rows)
    return jnp.where(near & real, 0.0, -1e30).astype(F32)


def forward_rows(b, dims, q_ref, k_ref, v_ref, g_ref, mixed_ref, dq_ref, bias):
    frames, rows, cols, slots, _, _ = dims
    own = BR * cols
    span = (BR + 2 * PAD) * cols
    width = NHG * HD
    count = k_ref.shape[2] // width
    n = frames * own
    mine = pl.ds(pl.multiple_of((b + 1) * own, own), own)
    inner = pl.ds(pl.multiple_of(b * own, own), own)
    wide = pl.ds(pl.multiple_of(b * own, own), span)
    state = {}

    def scores(g):
        at = pl.ds(g * width, width)
        q = stack_heads(q_ref[:frames, mine, at].reshape(n, width))
        gr = stack_heads(g_ref[:frames, mine, at].reshape(n, width))
        k = k_ref[:, wide, at].reshape(slots * span, width)
        v = v_ref[:, wide, at].reshape(slots * span, width)
        state[g] = [gr, dot_nt(q, k), dot_nt(gr, v)]

    def soft(g):
        s = state[g][1]
        s = (s.reshape(NHG, n, slots * span) + bias[None]).reshape(NHG * n, slots * span)
        top = jnp.max(s, axis=1, keepdims=True)
        e = jnp.exp(s - top)
        total = jnp.sum(e, axis=1, keepdims=True)
        state[g] += [e * (1.0 / total), top + jnp.log(total)]

    def mix(g):
        at = pl.ds(g * width, width)
        v = v_ref[:, wide, at].reshape(slots * span, width)
        mixed = dot_nn(state[g][3].astype(BF), v).astype(BF)
        state[g].append(mixed)
        mixed_ref[:, inner, at] = pick_heads(mixed).reshape(frames, own, width)

    def grads(g, stat):
        at = pl.ds(g * width, width)
        gr, _, dp, p, lse, mixed = state.pop(g)
        delta = jnp.sum(gr.astype(F32) * mixed.astype(F32), axis=1, keepdims=True)
        ds = (p * (dp - delta)).astype(BF)
        k = k_ref[:, wide, at].reshape(slots * span, width)
        dq = pick_heads(dot_nn(ds, k)) * HD ** (-0.5)
        dq_ref[:, inner, at] = dq.astype(BF).reshape(frames, own, width)
        lane = lax.broadcasted_iota(jnp.int32, (n, 128), 1)
        for h in range(NHG):
            stat = jnp.where(lane == g * NHG + h, lse[h * n : (h + 1) * n], stat)
            stat = jnp.where(lane == 64 + g * NHG + h, delta[h * n : (h + 1) * n], stat)
        return stat

    stat = jnp.zeros((n, 128), F32)
    scores(0)
    scores(1)
    soft(0)
    for g in range(count):
        if g + 2 < count:
            scores(g + 2)
        mix(g)
        if g + 1 < count:
            soft(g + 1)
        stat = grads(g, stat)
    return stat.reshape(frames, own, 128)


def backward_rows(b, dims, q_ref, k_ref, v_ref, g_ref, dk_ref, dv_ref, flip, bias):
    frames, rows, cols, slots, _, _ = dims
    own = BR * cols
    span = (BR + 2 * PAD) * cols
    width = NHG * HD
    count = k_ref.shape[2] // width
    n = frames * own
    full = (NHG, n, slots * span)
    mine = pl.ds(pl.multiple_of((b + 1) * own, own), own)
    inner = pl.ds(pl.multiple_of(b * own, own), own)
    wide = pl.ds(pl.multiple_of(b * own, own), span)
    state = {}

    def scores(g):
        at = pl.ds(g * width, width)
        k = stack_heads(k_ref[:frames, mine, at].reshape(n, width))
        v = stack_heads(v_ref[:frames, mine, at].reshape(n, width))
        q = q_ref[:, wide, at].reshape(slots * span, width)
        gr = g_ref[:, wide, at].reshape(slots * span, width)
        state[g] = [dot_nt(k, q), dot_nt(v, gr)]

    def soft(g):
        s, dp = state[g]
        lse = flip[g * NHG : (g + 1) * NHG, :]
        delta = flip[64 + g * NHG : 64 + (g + 1) * NHG, :]
        p = jnp.exp(s.reshape(full) + bias[None] - lse[:, None, :])
        ds = p * (dp.reshape(full) - delta[:, None, :])
        state[g] = [p.astype(BF).reshape(NHG * n, -1), ds.astype(BF).reshape(NHG * n, -1)]

    def grads(g):
        at = pl.ds(g * width, width)
        p, ds = state.pop(g)
        q = q_ref[:, wide, at].reshape(slots * span, width)
        gr = g_ref[:, wide, at].reshape(slots * span, width)
        dv_ref[:, inner, at] = pick_heads(dot_nn(p, gr)).astype(BF).reshape(frames, own, width)
        dk_ref[:, inner, at] = pick_heads(dot_nn(ds, q)).astype(BF).reshape(frames, own, width)

    scores(0)
    scores(1)
    soft(0)
    for g in range(count):
        if g + 2 < count:
            scores(g + 2)
        if g + 1 < count:
            soft(g + 1)
        grads(g)


def project(src_ref, jobs, slots, spans):
    width = src_ref.shape[2]
    tile = 256
    first, count = slots
    some = pl.ds(first, count)
    total = sum(size for _, size in spans)

    def step(i, _):
        at = pl.ds(pl.multiple_of(i * tile, tile), tile)
        parts = [src_ref[some, a : a + size, :].reshape(count * size, width) for a, size in spans]
        rows = parts[0] if len(parts) == 1 else jnp.concatenate(parts, axis=0)
        for w_ref, dst_ref, flip, factor in jobs:
            out = dot_nt(rows, w_ref[at, :]) if flip else dot_nn(rows, w_ref[:, at])
            out = out.astype(BF)
            if factor != 1:
                out = out * jnp.asarray(factor, BF)
            begin = 0
            for a, size in spans:
                piece = out[begin : begin + count * size]
                if len(dst_ref.shape) == 4:
                    dst_ref[some, :, :, at] = piece.reshape(count, *dst_ref.shape[1:3], tile)
                else:
                    dst_ref[some, a : a + size, at] = piece.reshape(count, size, tile)
                begin += count * size
        return 0

    lax.fori_loop(0, width // tile, step, 0)


class Exchange:
    def __init__(self, ref, sems, dims, edge):
        frames, rows, cols, slots, tm, height = dims
        self.ref, self.edge, self.frames = ref, edge, frames
        self.t, self.h = lax.axis_index("tm"), lax.axis_index("height")
        self.tm, self.height = tm, height
        self.send_x, self.recv_x, self.send_h, self.recv_h = sems
        tokens = rows * cols
        self.pieces = [(edge, edge), (tokens, edge), (2 * edge, tokens - 2 * edge)]
        self.groups = slots // frames

    def links(self):
        if self.tm == 2:
            return [(1, 1 - self.t, None, None)]
        return [
            (1, self.t + 1, self.t < self.tm - 1, self.t > 0),
            (2, self.t - 1, self.t > 0, self.t < self.tm - 1),
        ]

    def tm_copy(self, link, piece):
        group, target, _, _ = self.links()[link]
        start, size = self.pieces[piece]
        rows = pl.ds(start, size)
        return pltpu.make_async_remote_copy(
            src_ref=self.ref.at[pl.ds(0, self.frames), rows],
            dst_ref=self.ref.at[pl.ds(group * self.frames, self.frames), rows],
            send_sem=self.send_x.at[link * 3 + piece],
            recv_sem=self.recv_x.at[link * 3 + piece],
            device_id=(target, self.h),
            device_id_type=pl.DeviceIdType.MESH,
        )

    def row_copy(self, group, up):
        low, high = self.pieces[0][0], self.pieces[1][0]
        end = high + self.edge
        some = pl.ds(group * self.frames, self.frames)
        src, dst = (high, 0) if up else (low, end)
        slot = group * 2 + int(up)
        return pltpu.make_async_remote_copy(
            src_ref=self.ref.at[some, pl.ds(src, self.edge)],
            dst_ref=self.ref.at[some, pl.ds(dst, self.edge)],
            send_sem=self.send_h.at[slot],
            recv_sem=self.recv_h.at[slot],
            device_id=(self.t, self.h + 1 if up else self.h - 1),
            device_id_type=pl.DeviceIdType.MESH,
        )

    def when(self, cond, act):
        if cond is None:
            act()
        else:
            pl.when(cond)(act)

    def clear(self):
        low, end = self.edge, self.pieces[1][0] + self.edge
        shape = self.ref.shape

        @pl.when(self.h == 0)
        def _():
            self.ref[:, 0:low, :] = jnp.zeros((shape[0], low, shape[2]), self.ref.dtype)

        @pl.when(self.h == self.height - 1)
        def _():
            self.ref[:, end:, :] = jnp.zeros((shape[0], low, shape[2]), self.ref.dtype)

        for group, _, _, there in self.links():
            if there is not None:

                @pl.when(jnp.logical_not(there))
                def _(group=group):
                    some = pl.ds(group * self.frames, self.frames)
                    self.ref[some, low:end, :] = jnp.zeros((self.frames, end - low, shape[2]), self.ref.dtype)

    def there(self, group):
        return None if group == 0 else self.links()[group - 1][3]

    def both(self, a, b):
        return b if a is None else a & b

    def send_tm(self):
        for piece in range(3):
            for link, (_, _, sends, _) in enumerate(self.links()):
                self.when(sends, lambda link=link, piece=piece: self.tm_copy(link, piece).start())

    def got_tm(self, pieces):
        for link, (_, _, _, gets) in enumerate(self.links()):
            for piece in pieces:
                self.when(gets, lambda link=link, piece=piece: self.tm_copy(link, piece).wait_recv())

    def send_rows(self, groups):
        for group in groups:
            there = self.there(group)
            self.when(self.both(there, self.h < self.height - 1), lambda g=group: self.row_copy(g, True).start())
            self.when(self.both(there, self.h > 0), lambda g=group: self.row_copy(g, False).start())

    def got_rows(self, groups):
        for group in groups:
            there = self.there(group)
            self.when(self.both(there, self.h > 0), lambda g=group: self.row_copy(g, True).wait_recv())
            self.when(self.both(there, self.h < self.height - 1), lambda g=group: self.row_copy(g, False).wait_recv())

    def sent(self):
        for piece in range(3):
            for link, (_, _, sends, _) in enumerate(self.links()):
                self.when(sends, lambda link=link, piece=piece: self.tm_copy(link, piece).wait_send())
        for group in range(self.groups):
            there = self.there(group)
            self.when(self.both(there, self.h < self.height - 1), lambda g=group: self.row_copy(g, True).wait_send())
            self.when(self.both(there, self.h > 0), lambda g=group: self.row_copy(g, False).wait_send())


def meet(dims):
    _, _, _, _, tm, height = dims
    t, h = lax.axis_index("tm"), lax.axis_index("height")
    barrier = pltpu.get_barrier_semaphore()
    count = jnp.int32(0)
    others = [(h > 0, t, h - 1), (h < height - 1, t, h + 1)]
    if tm == 2:
        pl.semaphore_signal(barrier, inc=1, device_id=(1 - t, h), device_id_type=pl.DeviceIdType.MESH)
        count = count + 1
    else:
        others += [(t > 0, t - 1, h), (t < tm - 1, t + 1, h)]
    for cond, tt, hh in others:

        @pl.when(cond)
        def _(tt=tt, hh=hh):
            pl.semaphore_signal(barrier, inc=1, device_id=(tt, hh), device_id_type=pl.DeviceIdType.MESH)

        count = count + cond.astype(jnp.int32)
    pl.semaphore_wait(barrier, count)


def kernel(
    dims, x_hbm, go_hbm, wq_hbm, wk_hbm, wv_hbm, wo_hbm,
    attended_ref, out_ref,
    x_ref, go_ref, q_ref, k_ref, v_ref, g_ref, wq_ref, wk_ref, wv_ref, wo_ref,
    mixed_ref, dq_ref, dk_ref, dv_ref, stat_ref, bias_ref, x4_ref, go4_ref, local_sem,
    *sems,
):
    frames, rows, cols, slots, tm, height = dims
    width = x_ref.shape[2]
    own = BR * cols
    span = (BR + 2 * PAD) * cols
    edge = PAD * cols
    tokens = rows * cols
    blocks = rows // BR
    scale = HD ** (-0.5)
    mid = pl.ds(edge, tokens)
    loads = [
        pltpu.make_async_copy(x_hbm, x4_ref, local_sem.at[0]),
        pltpu.make_async_copy(go_hbm, go4_ref, local_sem.at[1]),
        pltpu.make_async_copy(wq_hbm, wq_ref, local_sem.at[2]),
        pltpu.make_async_copy(wk_hbm, wk_ref, local_sem.at[3]),
        pltpu.make_async_copy(wv_hbm, wv_ref, local_sem.at[4]),
        pltpu.make_async_copy(wo_hbm, wo_ref, local_sem.at[5]),
    ]
    for load in loads:
        load.start()
    ex_x = Exchange(x_ref, sems[0:4], dims, edge)
    ex_go = Exchange(go_ref, sems[4:8], dims, edge)
    ex_st = Exchange(stat_ref, sems[8:12], dims, edge)
    loads[0].wait()
    x_ref[pl.ds(0, frames), mid, :] = x4_ref[...].reshape(frames, tokens, width)
    meet(dims)
    ex_x.send_tm()
    ex_x.send_rows([0])
    loads[1].wait()
    go_ref[pl.ds(0, frames), mid, :] = go4_ref[...].reshape(frames, tokens, width)
    ex_go.send_rows([0])
    ex_x.clear()
    ex_go.clear()
    ex_st.clear()

    def fill(b, _):
        bias_ref[b] = make_bias(b, dims)
        return 0

    lax.fori_loop(0, blocks, fill, 0)
    centre = [(edge, tokens)]
    rims = [(0, edge), (edge + tokens, edge)]
    for load in loads[2:5]:
        load.wait()
    to_q = (wq_ref, q_ref, False, scale)
    to_k = (wk_ref, k_ref, False, 1)
    to_v = (wv_ref, v_ref, False, 1)
    to_g = (wo_ref, g_ref, True, 1)
    project(x_ref, [to_q, to_k, to_v], (0, frames), centre)
    loads[5].wait()
    project(go_ref, [to_g], (0, frames), centre)
    ex_x.got_rows([0])
    project(x_ref, [to_q, to_k, to_v], (0, frames), rims)
    ex_go.got_rows([0])
    project(go_ref, [to_g], (0, frames), rims)

    def forward(b):
        stat = forward_rows(b, dims, q_ref, k_ref, v_ref, g_ref, mixed_ref, dq_ref, bias_ref[b])
        at = pl.ds(pl.multiple_of((b + 1) * own, own), own)
        stat_ref[pl.ds(0, frames), at, :] = stat

    def backward(b):
        at = pl.ds(pl.multiple_of(b * own, own), span)
        flip = stat_ref[:, at, :].reshape(slots * span, 128).T
        backward_rows(b, dims, q_ref, k_ref, v_ref, g_ref, dk_ref, dv_ref, flip, bias_ref[b])

    def inner_blocks(act):
        def step(b, _):
            act(b)
            return 0

        lax.fori_loop(1, blocks - 1, step, 0)

    def outer_blocks(act):
        def step(i, _):
            act(i * (blocks - 1))
            return 0

        lax.fori_loop(0, 2, step, 0)

    others = list(range(1, slots // frames))
    ex_x.got_tm([0, 1])
    ex_x.send_rows(others)
    ex_x.got_tm([2])
    ex_go.send_tm()
    ex_x.got_rows(others)
    rest = (frames, slots - frames)
    project(x_ref, [to_k, to_v], rest, centre + rims)
    inner_blocks(forward)
    ex_go.got_tm([0, 1])
    ex_go.send_rows(others)
    outer_blocks(forward)
    ex_st.send_tm()
    ex_st.send_rows([0])
    project(mixed_ref, [(wo_ref, attended_ref, False, 1)], (0, frames), [(0, tokens)])
    ex_go.got_tm([2])
    project(x_ref, [to_q], rest, centre + rims)
    ex_st.got_tm([0, 1])
    ex_st.send_rows(others)
    ex_go.got_rows(others)
    project(go_ref, [to_g], rest, centre + rims)
    ex_st.got_tm([2])
    inner_blocks(backward)
    ex_st.got_rows([0] + others)
    outer_blocks(backward)
    tile = 256

    def out_step(i, _):
        at = pl.ds(pl.multiple_of(i * tile, tile), tile)
        total = dot_nt(dq_ref[...].reshape(frames * tokens, width), wq_ref[at, :])
        total += dot_nt(dk_ref[...].reshape(frames * tokens, width), wk_ref[at, :])
        total += dot_nt(dv_ref[...].reshape(frames * tokens, width), wv_ref[at, :])
        out_ref[:, :, :, at] = total.astype(BF).reshape(frames, rows, cols, tile)
        return 0

    lax.fori_loop(0, width // tile, out_step, 0)
    ex_x.sent()
    ex_go.sent()
    ex_st.sent()


def copy_kernel(a_hbm, b_hbm, a_out, b_out, sem):
    copies = []
    for i, (src, dst) in enumerate(((a_hbm, a_out), (b_hbm, b_out))):
        parts = 4 * src.shape[0]
        rows = src.shape[1] // 4
        for part in range(parts):
            at = (part // 4, pl.ds(part % 4 * rows, rows))
            copies.append(pltpu.make_async_copy(src.at[at], dst.at[at], sem.at[i * parts + part]))
    for copy in copies:
        copy.start()
    for copy in copies:
        copy.wait()


def shards(inputs, w_query, w_key, w_value, w_out, grad_out):
    frames, rows, cols, width = inputs.shape
    tm, height = lax.axis_size("tm"), lax.axis_size("height")
    groups = 2 if tm == 2 else 3
    slots = groups * frames
    dims = (frames, rows, cols, slots, tm, height)
    tokens = rows * cols
    wide = tokens + 2 * PAD * cols
    keys = slots * (BR + 2 * PAD) * cols
    mine = frames * BR * cols
    vmem = pl.BlockSpec(memory_space=pltpu.VMEM)
    hbm = pl.BlockSpec(memory_space=pl.ANY)
    links = 3 * (groups - 1)
    sems = [pltpu.SemaphoreType.DMA((links,))] * 2 + [pltpu.SemaphoreType.DMA((2 * groups,))] * 2
    both = pl.pallas_call(
        functools.partial(kernel, dims),
        out_shape=[jax.ShapeDtypeStruct(inputs.shape, BF)] * 2,
        in_specs=[hbm] * 6,
        out_specs=[vmem] * 2,
        scratch_shapes=[pltpu.VMEM((slots, wide, width), BF)] * 6
        + [pltpu.VMEM((width, width), BF)] * 4
        + [pltpu.VMEM((frames, tokens, width), BF)] * 4
        + [
            pltpu.VMEM((slots, wide, 128), F32),
            pltpu.VMEM((rows // BR, mine, keys), F32),
            pltpu.VMEM(inputs.shape, BF),
            pltpu.VMEM(inputs.shape, BF),
            pltpu.SemaphoreType.DMA((6,)),
        ]
        + sems * 3,
        compiler_params=pltpu.CompilerParams(
            vmem_limit_bytes=56 * 1024 * 1024, collective_id=0, has_side_effects=True
        ),
        name="attention",
    )(inputs, grad_out, w_query, w_key, w_value, w_out)
    return pl.pallas_call(
        copy_kernel,
        out_shape=[jax.ShapeDtypeStruct(inputs.shape, BF)] * 2,
        in_specs=[hbm] * 2,
        out_specs=[hbm] * 2,
        scratch_shapes=[pltpu.SemaphoreType.DMA((8 * frames,))],
        name="copy_out",
    )(*both)


def solution(mesh):
    placed = (P("tm", "height", None, None), P(), P(), P(), P(), P("tm", "height", None, None))
    return jax.shard_map(
        shards,
        mesh=mesh,
        in_specs=placed,
        out_specs=(P("tm", "height", None, None), P("tm", "height", None, None)),
        check_vma=False,
    )
```

```python
import functools

import jax
import jax.numpy as jnp
from jax import lax
from jax.experimental import pallas as pl
from jax.experimental.pallas import tpu as pltpu
from jax.sharding import PartitionSpec as P

HD = 64
RT = 2
RH = 7
RW = 7
PAD = 8
BR = 8
NHG = 4
BF = jnp.bfloat16
F32 = jnp.float32


def dot_nn(a, b):
    return jnp.dot(a, b, preferred_element_type=F32)


def dot_nt(a, b):
    return lax.dot_general(a, b, (((1,), (1,)), ((), ())), preferred_element_type=F32)


def stack_heads(a, mask_ref):
    return (a[None] * mask_ref[...]).reshape(NHG * a.shape[0], a.shape[1])


def pick_heads(a):
    n = a.shape[0] // NHG
    head = lax.broadcasted_iota(jnp.int32, (n, a.shape[1]), 1) // HD
    out = a[:n]
    for h in range(1, NHG):
        out = jnp.where(head == h, a[h * n : (h + 1) * n], out)
    return out


def make_bias(block, dims):
    frames, rows, cols, slots, tm_size, height_size = dims
    t = lax.axis_index("tm")
    first = lax.axis_index("height") * rows
    span = (BR + 2 * PAD) * cols
    own = BR * cols
    shape = (frames * own, slots * span)
    i = lax.broadcasted_iota(jnp.int32, shape, 0)
    j = lax.broadcasted_iota(jnp.int32, shape, 1)
    qf = t * frames + i // own
    qr = (i % own) // cols
    slot = j // span
    kr = (j % span) // cols
    group = slot // frames
    if slots == 2 * frames:
        base = jnp.where(group == 0, t, 1 - t)
    else:
        base = jnp.where(group == 0, t, jnp.where(group == 1, t - 1, t + 1))
    kf = base * frames + slot % frames
    near = (jnp.abs(kf - qf) <= RT) & (jnp.abs(kr - PAD - qr) <= RH)
    row = first + block * BR + kr - PAD
    real = (kf >= 0) & (kf < tm_size * frames) & (row >= 0) & (row < height_size * rows)
    return jnp.where(near & real, 0.0, -1e30).astype(F32)


def forward_rows(b, dims, q_ref, k_ref, v_ref, g_ref, mixed_ref, dq_ref, bias, mask_ref):
    frames, rows, cols, slots, _, _ = dims
    own = BR * cols
    span = (BR + 2 * PAD) * cols
    width = NHG * HD
    count = k_ref.shape[2] // width
    n = frames * own
    mine = pl.ds(pl.multiple_of((b + 1) * own, own), own)
    inner = pl.ds(pl.multiple_of(b * own, own), own)
    wide = pl.ds(pl.multiple_of(b * own, own), span)
    state = {}

    def scores(g):
        at = pl.ds(g * width, width)
        q = stack_heads(q_ref[:frames, mine, at].reshape(n, width), mask_ref)
        gr = stack_heads(g_ref[:frames, mine, at].reshape(n, width), mask_ref)
        k = k_ref[:, wide, at].reshape(slots * span, width)
        v = v_ref[:, wide, at].reshape(slots * span, width)
        state[g] = [gr, dot_nt(q, k), dot_nt(gr, v)]

    def soft(g):
        s = state[g][1]
        s = (s.reshape(NHG, n, slots * span) + bias[None]).reshape(NHG * n, slots * span)
        top = jnp.max(s, axis=1, keepdims=True)
        e = jnp.exp(s - top)
        total = jnp.sum(e, axis=1, keepdims=True)
        state[g] += [e * (1.0 / total), top + jnp.log(total)]

    def mix(g):
        at = pl.ds(g * width, width)
        v = v_ref[:, wide, at].reshape(slots * span, width)
        mixed = dot_nn(state[g][3].astype(BF), v).astype(BF)
        state[g].append(mixed)
        mixed_ref[:, inner, at] = pick_heads(mixed).reshape(frames, own, width)

    def grads(g, stat):
        at = pl.ds(g * width, width)
        gr, _, dp, p, lse, mixed = state.pop(g)
        delta = jnp.sum(gr.astype(F32) * mixed.astype(F32), axis=1, keepdims=True)
        ds = (p * (dp - delta)).astype(BF)
        k = k_ref[:, wide, at].reshape(slots * span, width)
        dq = pick_heads(dot_nn(ds, k)) * HD ** (-0.5)
        dq_ref[:, inner, at] = dq.astype(BF).reshape(frames, own, width)
        lane = lax.broadcasted_iota(jnp.int32, (n, 128), 1)
        for h in range(NHG):
            stat = jnp.where(lane == g * NHG + h, lse[h * n : (h + 1) * n], stat)
            stat = jnp.where(lane == 64 + g * NHG + h, delta[h * n : (h + 1) * n], stat)
        return stat

    stat = jnp.zeros((n, 128), F32)
    scores(0)
    scores(1)
    soft(0)
    for g in range(count):
        if g + 2 < count:
            scores(g + 2)
        mix(g)
        if g + 1 < count:
            soft(g + 1)
        stat = grads(g, stat)
    return stat.reshape(frames, own, 128)


def backward_rows(b, dims, q_ref, k_ref, v_ref, g_ref, dk_ref, dv_ref, flip, bias, mask_ref):
    frames, rows, cols, slots, _, _ = dims
    own = BR * cols
    span = (BR + 2 * PAD) * cols
    width = NHG * HD
    count = k_ref.shape[2] // width
    n = frames * own
    full = (NHG, n, slots * span)
    mine = pl.ds(pl.multiple_of((b + 1) * own, own), own)
    inner = pl.ds(pl.multiple_of(b * own, own), own)
    wide = pl.ds(pl.multiple_of(b * own, own), span)
    state = {}

    def scores(g):
        at = pl.ds(g * width, width)
        k = stack_heads(k_ref[:frames, mine, at].reshape(n, width), mask_ref)
        v = stack_heads(v_ref[:frames, mine, at].reshape(n, width), mask_ref)
        q = q_ref[:, wide, at].reshape(slots * span, width)
        gr = g_ref[:, wide, at].reshape(slots * span, width)
        state[g] = [dot_nt(k, q), dot_nt(v, gr)]

    def soft(g):
        s, dp = state[g]
        lse = flip[g * NHG : (g + 1) * NHG, :]
        delta = flip[64 + g * NHG : 64 + (g + 1) * NHG, :]
        p = jnp.exp(s.reshape(full) + bias[None] - lse[:, None, :])
        ds = p * (dp.reshape(full) - delta[:, None, :])
        state[g] = [p.astype(BF).reshape(NHG * n, -1), ds.astype(BF).reshape(NHG * n, -1)]

    def grads(g):
        at = pl.ds(g * width, width)
        p, ds = state.pop(g)
        q = q_ref[:, wide, at].reshape(slots * span, width)
        gr = g_ref[:, wide, at].reshape(slots * span, width)
        dv_ref[:, inner, at] = pick_heads(dot_nn(p, gr)).astype(BF).reshape(frames, own, width)
        dk_ref[:, inner, at] = pick_heads(dot_nn(ds, q)).astype(BF).reshape(frames, own, width)

    scores(0)
    scores(1)
    soft(0)
    for g in range(count):
        if g + 2 < count:
            scores(g + 2)
        if g + 1 < count:
            soft(g + 1)
        grads(g)


def project(jobs):
    width = jobs[0][3].shape[0]
    tile = 256

    def step(i, _):
        at = pl.ds(pl.multiple_of(i * tile, tile), tile)
        for src_ref, (first, count), spans, w_ref, dst_ref, flip, factor in jobs:
            some = pl.ds(first, count)
            parts = [src_ref[some, a : a + size, :].reshape(count * size, width) for a, size in spans]
            rows = parts[0] if len(parts) == 1 else jnp.concatenate(parts, axis=0)
            out = dot_nt(rows, w_ref[at, :]) if flip else dot_nn(rows, w_ref[:, at])
            out = out.astype(BF)
            if factor != 1:
                out = out * jnp.asarray(factor, BF)
            begin = 0
            for a, size in spans:
                piece = out[begin : begin + count * size]
                if len(dst_ref.shape) == 4:
                    dst_ref[some, :, :, at] = piece.reshape(count, *dst_ref.shape[1:3], tile)
                else:
                    dst_ref[some, a : a + size, at] = piece.reshape(count, size, tile)
                begin += count * size
        return 0

    lax.fori_loop(0, width // tile, step, 0)


class Exchange:
    def __init__(self, ref, sems, dims, edge):
        frames, rows, cols, slots, tm, height = dims
        self.ref, self.edge, self.frames = ref, edge, frames
        self.t, self.h = lax.axis_index("tm"), lax.axis_index("height")
        self.tm, self.height = tm, height
        self.send_x, self.recv_x, self.send_h, self.recv_h = sems
        tokens = rows * cols
        self.pieces = [(edge, edge), (tokens, edge), (2 * edge, tokens - 2 * edge)]
        self.groups = slots // frames

    def links(self):
        if self.tm == 2:
            return [(1, 1 - self.t, None, None)]
        return [
            (1, self.t + 1, self.t < self.tm - 1, self.t > 0),
            (2, self.t - 1, self.t > 0, self.t < self.tm - 1),
        ]

    def tm_copy(self, link, piece):
        group, target, _, _ = self.links()[link]
        start, size = self.pieces[piece]
        rows = pl.ds(start, size)
        return pltpu.make_async_remote_copy(
            src_ref=self.ref.at[pl.ds(0, self.frames), rows],
            dst_ref=self.ref.at[pl.ds(group * self.frames, self.frames), rows],
            send_sem=self.send_x.at[link * 3 + piece],
            recv_sem=self.recv_x.at[link * 3 + piece],
            device_id=(target, self.h),
            device_id_type=pl.DeviceIdType.MESH,
        )

    def row_copy(self, group, up):
        low, high = self.pieces[0][0], self.pieces[1][0]
        end = high + self.edge
        some = pl.ds(group * self.frames, self.frames)
        src, dst = (high, 0) if up else (low, end)
        slot = group * 2 + int(up)
        return pltpu.make_async_remote_copy(
            src_ref=self.ref.at[some, pl.ds(src, self.edge)],
            dst_ref=self.ref.at[some, pl.ds(dst, self.edge)],
            send_sem=self.send_h.at[slot],
            recv_sem=self.recv_h.at[slot],
            device_id=(self.t, self.h + 1 if up else self.h - 1),
            device_id_type=pl.DeviceIdType.MESH,
        )

    def when(self, cond, act):
        if cond is None:
            act()
        else:
            pl.when(cond)(act)

    def clear(self):
        low, end = self.edge, self.pieces[1][0] + self.edge
        shape = self.ref.shape

        @pl.when(self.h == 0)
        def _():
            self.ref[:, 0:low, :] = jnp.zeros((shape[0], low, shape[2]), self.ref.dtype)

        @pl.when(self.h == self.height - 1)
        def _():
            self.ref[:, end:, :] = jnp.zeros((shape[0], low, shape[2]), self.ref.dtype)

        for group, _, _, there in self.links():
            if there is not None:

                @pl.when(jnp.logical_not(there))
                def _(group=group):
                    some = pl.ds(group * self.frames, self.frames)
                    self.ref[some, low:end, :] = jnp.zeros((self.frames, end - low, shape[2]), self.ref.dtype)

    def there(self, group):
        return None if group == 0 else self.links()[group - 1][3]

    def both(self, a, b):
        return b if a is None else a & b

    def send_tm(self):
        for piece in range(3):
            for link, (_, _, sends, _) in enumerate(self.links()):
                self.when(sends, lambda link=link, piece=piece: self.tm_copy(link, piece).start())

    def got_tm(self, pieces):
        for link, (_, _, _, gets) in enumerate(self.links()):
            for piece in pieces:
                self.when(gets, lambda link=link, piece=piece: self.tm_copy(link, piece).wait_recv())

    def send_rows(self, groups):
        for group in groups:
            there = self.there(group)
            self.when(self.both(there, self.h < self.height - 1), lambda g=group: self.row_copy(g, True).start())
            self.when(self.both(there, self.h > 0), lambda g=group: self.row_copy(g, False).start())

    def got_rows(self, groups):
        for group in groups:
            there = self.there(group)
            self.when(self.both(there, self.h > 0), lambda g=group: self.row_copy(g, True).wait_recv())
            self.when(self.both(there, self.h < self.height - 1), lambda g=group: self.row_copy(g, False).wait_recv())

    def sent(self):
        for piece in range(3):
            for link, (_, _, sends, _) in enumerate(self.links()):
                self.when(sends, lambda link=link, piece=piece: self.tm_copy(link, piece).wait_send())
        for group in range(self.groups):
            there = self.there(group)
            self.when(self.both(there, self.h < self.height - 1), lambda g=group: self.row_copy(g, True).wait_send())
            self.when(self.both(there, self.h > 0), lambda g=group: self.row_copy(g, False).wait_send())


def greet(dims):
    _, _, _, _, tm, height = dims
    t, h = lax.axis_index("tm"), lax.axis_index("height")
    barrier = pltpu.get_barrier_semaphore()
    count = jnp.int32(0)
    others = [(h > 0, t, h - 1), (h < height - 1, t, h + 1)]
    if tm == 2:
        pl.semaphore_signal(barrier, inc=1, device_id=(1 - t, h), device_id_type=pl.DeviceIdType.MESH)
        count = count + 1
    else:
        others += [(t > 0, t - 1, h), (t < tm - 1, t + 1, h)]
    for cond, tt, hh in others:

        @pl.when(cond)
        def _(tt=tt, hh=hh):
            pl.semaphore_signal(barrier, inc=1, device_id=(tt, hh), device_id_type=pl.DeviceIdType.MESH)

        count = count + cond.astype(jnp.int32)
    return count


def kernel(
    dims, x_hbm, go_hbm, wq_hbm, wk_hbm, wv_hbm, wo_hbm,
    attended_ref, out_ref,
    x_ref, go_ref, q_ref, k_ref, v_ref, g_ref, wq_ref, wk_ref, wv_ref, wo_ref,
    mixed_ref, dq_ref, dk_ref, dv_ref, stat_ref, bias_ref, x4_ref, go4_ref, mask_ref, local_sem,
    *sems,
):
    frames, rows, cols, slots, tm, height = dims
    width = x_ref.shape[2]
    own = BR * cols
    span = (BR + 2 * PAD) * cols
    edge = PAD * cols
    tokens = rows * cols
    blocks = rows // BR
    scale = HD ** (-0.5)
    mid = pl.ds(edge, tokens)
    loads = [
        pltpu.make_async_copy(x_hbm, x4_ref, local_sem.at[0]),
        pltpu.make_async_copy(go_hbm, go4_ref, local_sem.at[1]),
        pltpu.make_async_copy(wq_hbm, wq_ref, local_sem.at[2]),
        pltpu.make_async_copy(wk_hbm, wk_ref, local_sem.at[3]),
        pltpu.make_async_copy(wv_hbm, wv_ref, local_sem.at[4]),
        pltpu.make_async_copy(wo_hbm, wo_ref, local_sem.at[5]),
    ]
    for load in loads:
        load.start()
    ex_x = Exchange(x_ref, sems[0:4], dims, edge)
    ex_go = Exchange(go_ref, sems[4:8], dims, edge)
    ex_st = Exchange(stat_ref, sems[8:12], dims, edge)
    count = greet(dims)
    loads[0].wait()
    x_ref[pl.ds(0, frames), mid, :] = x4_ref[...].reshape(frames, tokens, width)
    pl.semaphore_wait(pltpu.get_barrier_semaphore(), count)
    ex_x.send_tm()
    ex_x.send_rows([0])
    loads[1].wait()
    go_ref[pl.ds(0, frames), mid, :] = go4_ref[...].reshape(frames, tokens, width)
    ex_go.send_rows([0])
    ex_x.clear()
    ex_go.clear()
    ex_st.clear()

    def fill(b, _):
        bias_ref[b] = make_bias(b, dims)
        return 0

    lax.fori_loop(0, blocks, fill, 0)
    head = lax.broadcasted_iota(jnp.int32, mask_ref.shape, 2) // HD
    mask_ref[...] = (head == lax.broadcasted_iota(jnp.int32, mask_ref.shape, 0)).astype(F32).astype(BF)
    centre = [(edge, tokens)]
    rims = [(0, edge), (edge + tokens, edge)]
    for load in loads[2:]:
        load.wait()

    def to_q(slots, spans):
        return (x_ref, slots, spans, wq_ref, q_ref, False, scale)

    def to_k(slots, spans):
        return (x_ref, slots, spans, wk_ref, k_ref, False, 1)

    def to_v(slots, spans):
        return (x_ref, slots, spans, wv_ref, v_ref, False, 1)

    def to_g(slots, spans):
        return (go_ref, slots, spans, wo_ref, g_ref, True, 1)

    first = (0, frames)
    rest = (frames, slots - frames)
    project([make(first, centre) for make in (to_q, to_k, to_v, to_g)])
    ex_x.got_rows([0])
    ex_go.got_rows([0])
    project([make(first, rims) for make in (to_q, to_k, to_v, to_g)])

    def forward(b):
        stat = forward_rows(b, dims, q_ref, k_ref, v_ref, g_ref, mixed_ref, dq_ref, bias_ref[b], mask_ref)
        at = pl.ds(pl.multiple_of((b + 1) * own, own), own)
        stat_ref[pl.ds(0, frames), at, :] = stat

    def backward(b):
        at = pl.ds(pl.multiple_of(b * own, own), span)
        flip = stat_ref[:, at, :].reshape(slots * span, 128).T
        backward_rows(b, dims, q_ref, k_ref, v_ref, g_ref, dk_ref, dv_ref, flip, bias_ref[b], mask_ref)

    def inner_blocks(act):
        def step(b, _):
            act(b)
            return 0

        lax.fori_loop(1, blocks - 1, step, 0)

    def outer_blocks(act):
        def step(i, _):
            act(i * (blocks - 1))
            return 0

        lax.fori_loop(0, 2, step, 0)

    others = list(range(1, slots // frames))
    ex_x.got_tm([0, 1])
    ex_x.send_rows(others)
    ex_x.got_tm([2])
    ex_go.send_tm()
    ex_x.got_rows(others)
    project([to_k(rest, centre + rims), to_v(rest, centre + rims)])
    inner_blocks(forward)
    ex_go.got_tm([0, 1])
    ex_go.send_rows(others)
    outer_blocks(forward)
    ex_st.send_tm()
    ex_st.send_rows([0])
    ex_go.got_tm([2])
    ex_go.got_rows(others)
    project([
        to_q(rest, centre + rims),
        to_g(rest, centre + rims),
        (mixed_ref, first, [(0, tokens)], wo_ref, attended_ref, False, 1),
    ])
    ex_st.got_tm([0, 1])
    ex_st.send_rows(others)
    ex_st.got_tm([2])
    inner_blocks(backward)
    ex_st.got_rows([0] + others)
    outer_blocks(backward)
    tile = 256

    def out_step(i, _):
        at = pl.ds(pl.multiple_of(i * tile, tile), tile)
        total = dot_nt(dq_ref[...].reshape(frames * tokens, width), wq_ref[at, :])
        total += dot_nt(dk_ref[...].reshape(frames * tokens, width), wk_ref[at, :])
        total += dot_nt(dv_ref[...].reshape(frames * tokens, width), wv_ref[at, :])
        out_ref[:, :, :, at] = total.astype(BF).reshape(frames, rows, cols, tile)
        return 0

    lax.fori_loop(0, width // tile, out_step, 0)
    ex_x.sent()
    ex_go.sent()
    ex_st.sent()


def copy_kernel(a_hbm, b_hbm, a_out, b_out, held_ref, in_sem, out_sem):
    arrive, leave = [], []
    for i, (src, dst) in enumerate(((a_hbm, a_out), (b_hbm, b_out))):
        for f in range(src.shape[0]):
            slot = i * src.shape[0] + f
            arrive.append(pltpu.make_async_copy(src.at[f], held_ref.at[slot], in_sem.at[slot]))
            leave.append(pltpu.make_async_copy(held_ref.at[slot], dst.at[f], out_sem.at[slot]))
    for copy in arrive:
        copy.start()
    for before, after in zip(arrive, leave):
        before.wait()
        after.start()
    for copy in leave:
        copy.wait()


def shards(inputs, w_query, w_key, w_value, w_out, grad_out):
    frames, rows, cols, width = inputs.shape
    tm, height = lax.axis_size("tm"), lax.axis_size("height")
    groups = 2 if tm == 2 else 3
    slots = groups * frames
    dims = (frames, rows, cols, slots, tm, height)
    tokens = rows * cols
    wide = tokens + 2 * PAD * cols
    keys = slots * (BR + 2 * PAD) * cols
    mine = frames * BR * cols
    vmem = pl.BlockSpec(memory_space=pltpu.VMEM)
    hbm = pl.BlockSpec(memory_space=pl.ANY)
    links = 3 * (groups - 1)
    sems = [pltpu.SemaphoreType.DMA((links,))] * 2 + [pltpu.SemaphoreType.DMA((2 * groups,))] * 2
    both = pl.pallas_call(
        functools.partial(kernel, dims),
        out_shape=[jax.ShapeDtypeStruct(inputs.shape, BF)] * 2,
        in_specs=[hbm] * 6,
        out_specs=[vmem] * 2,
        scratch_shapes=[pltpu.VMEM((slots, wide, width), BF)] * 6
        + [pltpu.VMEM((width, width), BF)] * 4
        + [pltpu.VMEM((frames, tokens, width), BF)] * 4
        + [
            pltpu.VMEM((slots, wide, 128), F32),
            pltpu.VMEM((rows // BR, mine, keys), F32),
            pltpu.VMEM(inputs.shape, BF),
            pltpu.VMEM(inputs.shape, BF),
            pltpu.VMEM((NHG, mine, NHG * HD), BF),
            pltpu.SemaphoreType.DMA((6,)),
        ]
        + sems * 3,
        compiler_params=pltpu.CompilerParams(
            vmem_limit_bytes=56 * 1024 * 1024, collective_id=0, has_side_effects=True
        ),
        name="attention",
    )(inputs, grad_out, w_query, w_key, w_value, w_out)
    return pl.pallas_call(
        copy_kernel,
        out_shape=[jax.ShapeDtypeStruct(inputs.shape, BF)] * 2,
        in_specs=[hbm] * 2,
        out_specs=[hbm] * 2,
        scratch_shapes=[
            pltpu.VMEM((2 * frames, rows, cols, width), BF),
            pltpu.SemaphoreType.DMA((2 * frames,)),
            pltpu.SemaphoreType.DMA((2 * frames,)),
        ],
        name="copy_out",
    )(*both)


def solution(mesh):
    placed = (P("tm", "height", None, None), P(), P(), P(), P(), P("tm", "height", None, None))
    return jax.shard_map(
        shards,
        mesh=mesh,
        in_specs=placed,
        out_specs=(P("tm", "height", None, None), P("tm", "height", None, None)),
        check_vma=False,
    )
```

```python
import functools

import jax
import jax.numpy as jnp
from jax import lax
from jax.experimental import pallas as pl
from jax.experimental.pallas import tpu as pltpu
from jax.sharding import PartitionSpec as P

HD = 64
RT = 2
RH = 7
RW = 7
PAD = 8
BR = 8
NHG = 2
BF = jnp.bfloat16
F32 = jnp.float32


def dot_nn(a, b):
    return jnp.dot(a, b, preferred_element_type=F32)


def dot_nt(a, b):
    return lax.dot_general(a, b, (((1,), (1,)), ((), ())), preferred_element_type=F32)


def stack_heads(a, mask_ref):
    return (a[None] * mask_ref[...]).reshape(NHG * a.shape[0], a.shape[1])


def pick_heads(a):
    n = a.shape[0] // NHG
    head = lax.broadcasted_iota(jnp.int32, (n, a.shape[1]), 1) // HD
    out = a[:n]
    for h in range(1, NHG):
        out = jnp.where(head == h, a[h * n : (h + 1) * n], out)
    return out


def make_bias(block, dims):
    frames, rows, cols, slots, tm_size, height_size = dims
    t = lax.axis_index("tm")
    first = lax.axis_index("height") * rows
    span = (BR + 2 * PAD) * cols
    own = BR * cols
    shape = (frames * own, slots * span)
    i = lax.broadcasted_iota(jnp.int32, shape, 0)
    j = lax.broadcasted_iota(jnp.int32, shape, 1)
    qf = t * frames + i // own
    qr = (i % own) // cols
    slot = j // span
    kr = (j % span) // cols
    group = slot // frames
    if slots == 2 * frames:
        base = jnp.where(group == 0, t, 1 - t)
    else:
        base = jnp.where(group == 0, t, jnp.where(group == 1, t - 1, t + 1))
    kf = base * frames + slot % frames
    near = (jnp.abs(kf - qf) <= RT) & (jnp.abs(kr - PAD - qr) <= RH)
    row = first + block * BR + kr - PAD
    real = (kf >= 0) & (kf < tm_size * frames) & (row >= 0) & (row < height_size * rows)
    return jnp.where(near & real, 0.0, -1e30).astype(F32)


def forward_rows(b, dims, q_ref, k_ref, v_ref, g_ref, mixed_ref, dq_ref, bias, mask_ref):
    frames, rows, cols, slots, _, _ = dims
    own = BR * cols
    span = (BR + 2 * PAD) * cols
    width = NHG * HD
    count = k_ref.shape[2] // width
    n = frames * own
    mine = pl.ds(pl.multiple_of((b + 1) * own, own), own)
    inner = pl.ds(pl.multiple_of(b * own, own), own)
    wide = pl.ds(pl.multiple_of(b * own, own), span)
    state = {}

    def scores(g):
        at = pl.ds(g * width, width)
        q = stack_heads(q_ref[:frames, mine, at].reshape(n, width), mask_ref)
        gr = stack_heads(g_ref[:frames, mine, at].reshape(n, width), mask_ref)
        k = k_ref[:, wide, at].reshape(slots * span, width)
        v = v_ref[:, wide, at].reshape(slots * span, width)
        state[g] = [gr, dot_nt(q, k), dot_nt(gr, v)]

    def soft(g):
        s = state[g][1]
        s = (s.reshape(NHG, n, slots * span) + bias[None]).reshape(NHG * n, slots * span)
        top = jnp.max(s, axis=1, keepdims=True)
        e = jnp.exp(s - top)
        total = jnp.sum(e, axis=1, keepdims=True)
        state[g] += [e * (1.0 / total), top + jnp.log(total)]

    def mix(g):
        at = pl.ds(g * width, width)
        v = v_ref[:, wide, at].reshape(slots * span, width)
        mixed = dot_nn(state[g][3].astype(BF), v).astype(BF)
        state[g].append(mixed)
        mixed_ref[:, inner, at] = pick_heads(mixed).reshape(frames, own, width)

    def grads(g, stat):
        at = pl.ds(g * width, width)
        gr, _, dp, p, lse, mixed = state.pop(g)
        delta = jnp.sum(gr.astype(F32) * mixed.astype(F32), axis=1, keepdims=True)
        ds = (p * (dp - delta)).astype(BF)
        k = k_ref[:, wide, at].reshape(slots * span, width)
        dq = pick_heads(dot_nn(ds, k)) * HD ** (-0.5)
        dq_ref[:, inner, at] = dq.astype(BF).reshape(frames, own, width)
        lane = lax.broadcasted_iota(jnp.int32, (n, 128), 1)
        for h in range(NHG):
            stat = jnp.where(lane == g * NHG + h, lse[h * n : (h + 1) * n], stat)
            stat = jnp.where(lane == 64 + g * NHG + h, delta[h * n : (h + 1) * n], stat)
        return stat

    stat = jnp.zeros((n, 128), F32)
    scores(0)
    scores(1)
    soft(0)
    for g in range(count):
        if g + 2 < count:
            scores(g + 2)
        mix(g)
        if g + 1 < count:
            soft(g + 1)
        stat = grads(g, stat)
    return stat.reshape(frames, own, 128)


def backward_rows(b, dims, q_ref, k_ref, v_ref, g_ref, dk_ref, dv_ref, flip, bias, mask_ref):
    frames, rows, cols, slots, _, _ = dims
    own = BR * cols
    span = (BR + 2 * PAD) * cols
    width = NHG * HD
    count = k_ref.shape[2] // width
    n = frames * own
    full = (NHG, n, slots * span)
    mine = pl.ds(pl.multiple_of((b + 1) * own, own), own)
    inner = pl.ds(pl.multiple_of(b * own, own), own)
    wide = pl.ds(pl.multiple_of(b * own, own), span)
    state = {}

    def scores(g):
        at = pl.ds(g * width, width)
        k = stack_heads(k_ref[:frames, mine, at].reshape(n, width), mask_ref)
        v = stack_heads(v_ref[:frames, mine, at].reshape(n, width), mask_ref)
        q = q_ref[:, wide, at].reshape(slots * span, width)
        gr = g_ref[:, wide, at].reshape(slots * span, width)
        state[g] = [dot_nt(k, q), dot_nt(v, gr)]

    def soft(g):
        s, dp = state[g]
        lse = flip[g * NHG : (g + 1) * NHG, :]
        delta = flip[64 + g * NHG : 64 + (g + 1) * NHG, :]
        p = jnp.exp(s.reshape(full) + bias[None] - lse[:, None, :])
        ds = p * (dp.reshape(full) - delta[:, None, :])
        state[g] = [p.astype(BF).reshape(NHG * n, -1), ds.astype(BF).reshape(NHG * n, -1)]

    def grads(g):
        at = pl.ds(g * width, width)
        p, ds = state.pop(g)
        q = q_ref[:, wide, at].reshape(slots * span, width)
        gr = g_ref[:, wide, at].reshape(slots * span, width)
        dv_ref[:, inner, at] = pick_heads(dot_nn(p, gr)).astype(BF).reshape(frames, own, width)
        dk_ref[:, inner, at] = pick_heads(dot_nn(ds, q)).astype(BF).reshape(frames, own, width)

    scores(0)
    scores(1)
    soft(0)
    for g in range(count):
        if g + 2 < count:
            scores(g + 2)
        if g + 1 < count:
            soft(g + 1)
        grads(g)


def project(jobs):
    width = jobs[0][3].shape[0]
    tile = 256

    def step(i, _):
        at = pl.ds(pl.multiple_of(i * tile, tile), tile)
        for src_ref, (first, count), spans, w_ref, dst_ref, flip, factor in jobs:
            some = pl.ds(first, count)
            parts = [src_ref[some, a : a + size, :].reshape(count * size, width) for a, size in spans]
            rows = parts[0] if len(parts) == 1 else jnp.concatenate(parts, axis=0)
            out = dot_nt(rows, w_ref[at, :]) if flip else dot_nn(rows, w_ref[:, at])
            out = out.astype(BF)
            if factor != 1:
                out = out * jnp.asarray(factor, BF)
            begin = 0
            for a, size in spans:
                piece = out[begin : begin + count * size]
                if len(dst_ref.shape) == 4:
                    dst_ref[some, :, :, at] = piece.reshape(count, *dst_ref.shape[1:3], tile)
                else:
                    dst_ref[some, a : a + size, at] = piece.reshape(count, size, tile)
                begin += count * size
        return 0

    lax.fori_loop(0, width // tile, step, 0, unroll=2)


class Exchange:
    def __init__(self, ref, sems, dims, edge):
        frames, rows, cols, slots, tm, height = dims
        self.ref, self.edge, self.frames = ref, edge, frames
        self.t, self.h = lax.axis_index("tm"), lax.axis_index("height")
        self.tm, self.height = tm, height
        self.send_x, self.recv_x, self.send_h, self.recv_h = sems
        tokens = rows * cols
        self.pieces = [(edge, edge), (tokens, edge), (2 * edge, tokens - 2 * edge)]
        self.groups = slots // frames

    def links(self):
        if self.tm == 2:
            return [(1, 1 - self.t, None, None)]
        return [
            (1, self.t + 1, self.t < self.tm - 1, self.t > 0),
            (2, self.t - 1, self.t > 0, self.t < self.tm - 1),
        ]

    def tm_copy(self, link, piece):
        group, target, _, _ = self.links()[link]
        start, size = self.pieces[piece]
        rows = pl.ds(start, size)
        return pltpu.make_async_remote_copy(
            src_ref=self.ref.at[pl.ds(0, self.frames), rows],
            dst_ref=self.ref.at[pl.ds(group * self.frames, self.frames), rows],
            send_sem=self.send_x.at[link * 3 + piece],
            recv_sem=self.recv_x.at[link * 3 + piece],
            device_id=(target, self.h),
            device_id_type=pl.DeviceIdType.MESH,
        )

    def row_copy(self, group, up):
        low, high = self.pieces[0][0], self.pieces[1][0]
        end = high + self.edge
        some = pl.ds(group * self.frames, self.frames)
        src, dst = (high, 0) if up else (low, end)
        slot = group * 2 + int(up)
        return pltpu.make_async_remote_copy(
            src_ref=self.ref.at[some, pl.ds(src, self.edge)],
            dst_ref=self.ref.at[some, pl.ds(dst, self.edge)],
            send_sem=self.send_h.at[slot],
            recv_sem=self.recv_h.at[slot],
            device_id=(self.t, self.h + 1 if up else self.h - 1),
            device_id_type=pl.DeviceIdType.MESH,
        )

    def when(self, cond, act):
        if cond is None:
            act()
        else:
            pl.when(cond)(act)

    def clear(self):
        low, end = self.edge, self.pieces[1][0] + self.edge
        shape = self.ref.shape

        @pl.when(self.h == 0)
        def _():
            self.ref[:, 0:low, :] = jnp.zeros((shape[0], low, shape[2]), self.ref.dtype)

        @pl.when(self.h == self.height - 1)
        def _():
            self.ref[:, end:, :] = jnp.zeros((shape[0], low, shape[2]), self.ref.dtype)

        for group, _, _, there in self.links():
            if there is not None:

                @pl.when(jnp.logical_not(there))
                def _(group=group):
                    some = pl.ds(group * self.frames, self.frames)
                    self.ref[some, low:end, :] = jnp.zeros((self.frames, end - low, shape[2]), self.ref.dtype)

    def there(self, group):
        return None if group == 0 else self.links()[group - 1][3]

    def both(self, a, b):
        return b if a is None else a & b

    def send_tm(self):
        for piece in range(3):
            for link, (_, _, sends, _) in enumerate(self.links()):
                self.when(sends, lambda link=link, piece=piece: self.tm_copy(link, piece).start())

    def got_tm(self, pieces):
        for link, (_, _, _, gets) in enumerate(self.links()):
            for piece in pieces:
                self.when(gets, lambda link=link, piece=piece: self.tm_copy(link, piece).wait_recv())

    def send_rows(self, groups):
        for group in groups:
            there = self.there(group)
            self.when(self.both(there, self.h < self.height - 1), lambda g=group: self.row_copy(g, True).start())
            self.when(self.both(there, self.h > 0), lambda g=group: self.row_copy(g, False).start())

    def got_rows(self, groups):
        for group in groups:
            there = self.there(group)
            self.when(self.both(there, self.h > 0), lambda g=group: self.row_copy(g, True).wait_recv())
            self.when(self.both(there, self.h < self.height - 1), lambda g=group: self.row_copy(g, False).wait_recv())

    def sent(self):
        for piece in range(3):
            for link, (_, _, sends, _) in enumerate(self.links()):
                self.when(sends, lambda link=link, piece=piece: self.tm_copy(link, piece).wait_send())
        for group in range(self.groups):
            there = self.there(group)
            self.when(self.both(there, self.h < self.height - 1), lambda g=group: self.row_copy(g, True).wait_send())
            self.when(self.both(there, self.h > 0), lambda g=group: self.row_copy(g, False).wait_send())


def greet(dims):
    _, _, _, _, tm, height = dims
    t, h = lax.axis_index("tm"), lax.axis_index("height")
    barrier = pltpu.get_barrier_semaphore()
    count = jnp.int32(0)
    others = [(h > 0, t, h - 1), (h < height - 1, t, h + 1)]
    if tm == 2:
        pl.semaphore_signal(barrier, inc=1, device_id=(1 - t, h), device_id_type=pl.DeviceIdType.MESH)
        count = count + 1
    else:
        others += [(t > 0, t - 1, h), (t < tm - 1, t + 1, h)]
    for cond, tt, hh in others:

        @pl.when(cond)
        def _(tt=tt, hh=hh):
            pl.semaphore_signal(barrier, inc=1, device_id=(tt, hh), device_id_type=pl.DeviceIdType.MESH)

        count = count + cond.astype(jnp.int32)
    return count


def kernel(
    dims, x_hbm, go_hbm, wq_hbm, wk_hbm, wv_hbm, wo_hbm,
    attended_ref, out_ref,
    x_ref, go_ref, q_ref, k_ref, v_ref, g_ref, wq_ref, wk_ref, wv_ref, wo_ref,
    mixed_ref, dq_ref, dk_ref, dv_ref, stat_ref, bias_ref, x4_ref, go4_ref, mask_ref, local_sem,
    *sems,
):
    frames, rows, cols, slots, tm, height = dims
    width = x_ref.shape[2]
    own = BR * cols
    span = (BR + 2 * PAD) * cols
    edge = PAD * cols
    tokens = rows * cols
    blocks = rows // BR
    scale = HD ** (-0.5)
    mid = pl.ds(edge, tokens)
    loads = [
        pltpu.make_async_copy(x_hbm, x4_ref, local_sem.at[0]),
        pltpu.make_async_copy(go_hbm, go4_ref, local_sem.at[1]),
        pltpu.make_async_copy(wq_hbm, wq_ref, local_sem.at[2]),
        pltpu.make_async_copy(wk_hbm, wk_ref, local_sem.at[3]),
        pltpu.make_async_copy(wv_hbm, wv_ref, local_sem.at[4]),
        pltpu.make_async_copy(wo_hbm, wo_ref, local_sem.at[5]),
    ]
    for load in loads:
        load.start()
    ex_x = Exchange(x_ref, sems[0:4], dims, edge)
    ex_go = Exchange(go_ref, sems[4:8], dims, edge)
    ex_st = Exchange(stat_ref, sems[8:12], dims, edge)
    count = greet(dims)
    loads[0].wait()
    x_ref[pl.ds(0, frames), mid, :] = x4_ref[...].reshape(frames, tokens, width)
    pl.semaphore_wait(pltpu.get_barrier_semaphore(), count)
    ex_x.send_tm()
    ex_x.send_rows([0])
    loads[1].wait()
    go_ref[pl.ds(0, frames), mid, :] = go4_ref[...].reshape(frames, tokens, width)
    ex_go.send_rows([0])
    ex_x.clear()
    ex_go.clear()
    ex_st.clear()

    def fill(b, _):
        bias_ref[b] = make_bias(b, dims)
        return 0

    lax.fori_loop(0, blocks, fill, 0)
    head = lax.broadcasted_iota(jnp.int32, mask_ref.shape, 2) // HD
    mask_ref[...] = (head == lax.broadcasted_iota(jnp.int32, mask_ref.shape, 0)).astype(F32).astype(BF)
    centre = [(edge, tokens)]
    rims = [(0, edge), (edge + tokens, edge)]
    for load in loads[2:]:
        load.wait()

    def to_q(slots, spans):
        return (x_ref, slots, spans, wq_ref, q_ref, False, scale)

    def to_k(slots, spans):
        return (x_ref, slots, spans, wk_ref, k_ref, False, 1)

    def to_v(slots, spans):
        return (x_ref, slots, spans, wv_ref, v_ref, False, 1)

    def to_g(slots, spans):
        return (go_ref, slots, spans, wo_ref, g_ref, True, 1)

    first = (0, frames)
    rest = (frames, slots - frames)
    project([make(first, centre) for make in (to_q, to_k, to_v, to_g)])
    ex_x.got_rows([0])
    ex_go.got_rows([0])
    project([make(first, rims) for make in (to_q, to_k, to_v, to_g)])

    def forward(b):
        stat = forward_rows(b, dims, q_ref, k_ref, v_ref, g_ref, mixed_ref, dq_ref, bias_ref[b], mask_ref)
        at = pl.ds(pl.multiple_of((b + 1) * own, own), own)
        stat_ref[pl.ds(0, frames), at, :] = stat

    def backward(b):
        at = pl.ds(pl.multiple_of(b * own, own), span)
        flip = stat_ref[:, at, :].reshape(slots * span, 128).T
        backward_rows(b, dims, q_ref, k_ref, v_ref, g_ref, dk_ref, dv_ref, flip, bias_ref[b], mask_ref)

    def inner_blocks(act):
        def step(b, _):
            act(b)
            return 0

        lax.fori_loop(1, blocks - 1, step, 0)

    def outer_blocks(act):
        def step(i, _):
            act(i * (blocks - 1))
            return 0

        lax.fori_loop(0, 2, step, 0)

    others = list(range(1, slots // frames))
    ex_x.got_tm([0, 1])
    ex_x.send_rows(others)
    edges = [(edge, edge), (tokens, edge)]
    project([to_k(rest, edges), to_v(rest, edges)])
    ex_x.got_tm([2])
    ex_go.send_tm()
    ex_x.got_rows(others)
    left = [(2 * edge, tokens - 2 * edge)] + rims
    project([to_k(rest, left), to_v(rest, left)])
    inner_blocks(forward)
    ex_go.got_tm([0, 1])
    ex_go.send_rows(others)
    outer_blocks(forward)
    ex_st.send_tm()
    ex_st.send_rows([0])
    ex_go.got_tm([2])
    ex_go.got_rows(others)
    project([
        to_q(rest, centre + rims),
        to_g(rest, centre + rims),
        (mixed_ref, first, [(0, tokens)], wo_ref, attended_ref, False, 1),
    ])
    ex_st.got_tm([0, 1])
    ex_st.send_rows(others)
    ex_st.got_tm([2])
    inner_blocks(backward)
    ex_st.got_rows([0] + others)
    outer_blocks(backward)
    tile = 256

    def out_step(i, _):
        at = pl.ds(pl.multiple_of(i * tile, tile), tile)
        total = dot_nt(dq_ref[...].reshape(frames * tokens, width), wq_ref[at, :])
        total += dot_nt(dk_ref[...].reshape(frames * tokens, width), wk_ref[at, :])
        total += dot_nt(dv_ref[...].reshape(frames * tokens, width), wv_ref[at, :])
        out_ref[:, :, :, at] = total.astype(BF).reshape(frames, rows, cols, tile)
        return 0

    lax.fori_loop(0, width // tile, out_step, 0, unroll=2)
    ex_x.sent()
    ex_go.sent()
    ex_st.sent()


def copy_kernel(a_hbm, b_hbm, a_out, b_out, held_ref, in_sem, out_sem):
    arrive, leave = [], []
    for i, (src, dst) in enumerate(((a_hbm, a_out), (b_hbm, b_out))):
        for f in range(src.shape[0]):
            slot = i * src.shape[0] + f
            arrive.append(pltpu.make_async_copy(src.at[f], held_ref.at[slot], in_sem.at[slot]))
            leave.append(pltpu.make_async_copy(held_ref.at[slot], dst.at[f], out_sem.at[slot]))
    for copy in arrive:
        copy.start()
    for before, after in zip(arrive, leave):
        before.wait()
        after.start()
    for copy in leave:
        copy.wait()


def shards(inputs, w_query, w_key, w_value, w_out, grad_out):
    frames, rows, cols, width = inputs.shape
    tm, height = lax.axis_size("tm"), lax.axis_size("height")
    groups = 2 if tm == 2 else 3
    slots = groups * frames
    dims = (frames, rows, cols, slots, tm, height)
    tokens = rows * cols
    wide = tokens + 2 * PAD * cols
    keys = slots * (BR + 2 * PAD) * cols
    mine = frames * BR * cols
    vmem = pl.BlockSpec(memory_space=pltpu.VMEM)
    hbm = pl.BlockSpec(memory_space=pl.ANY)
    links = 3 * (groups - 1)
    sems = [pltpu.SemaphoreType.DMA((links,))] * 2 + [pltpu.SemaphoreType.DMA((2 * groups,))] * 2
    both = pl.pallas_call(
        functools.partial(kernel, dims),
        out_shape=[jax.ShapeDtypeStruct(inputs.shape, BF)] * 2,
        in_specs=[hbm] * 6,
        out_specs=[vmem] * 2,
        scratch_shapes=[pltpu.VMEM((slots, wide, width), BF)] * 6
        + [pltpu.VMEM((width, width), BF)] * 4
        + [pltpu.VMEM((frames, tokens, width), BF)] * 4
        + [
            pltpu.VMEM((slots, wide, 128), F32),
            pltpu.VMEM((rows // BR, mine, keys), F32),
            pltpu.VMEM(inputs.shape, BF),
            pltpu.VMEM(inputs.shape, BF),
            pltpu.VMEM((NHG, mine, NHG * HD), BF),
            pltpu.SemaphoreType.DMA((6,)),
        ]
        + sems * 3,
        compiler_params=pltpu.CompilerParams(
            vmem_limit_bytes=56 * 1024 * 1024, collective_id=0, has_side_effects=True
        ),
        name="attention",
    )(inputs, grad_out, w_query, w_key, w_value, w_out)
    return pl.pallas_call(
        copy_kernel,
        out_shape=[jax.ShapeDtypeStruct(inputs.shape, BF)] * 2,
        in_specs=[hbm] * 2,
        out_specs=[hbm] * 2,
        scratch_shapes=[
            pltpu.VMEM((2 * frames, rows, cols, width), BF),
            pltpu.SemaphoreType.DMA((2 * frames,)),
            pltpu.SemaphoreType.DMA((2 * frames,)),
        ],
        name="copy_out",
    )(*both)


def solution(mesh):
    placed = (P("tm", "height", None, None), P(), P(), P(), P(), P("tm", "height", None, None))
    return jax.shard_map(
        shards,
        mesh=mesh,
        in_specs=placed,
        out_specs=(P("tm", "height", None, None), P("tm", "height", None, None)),
        check_vma=False,
    )
```

```python
import functools

import jax
import jax.numpy as jnp
from jax import lax
from jax.experimental import pallas as pl
from jax.experimental.pallas import tpu as pltpu
from jax.sharding import PartitionSpec as P

HD = 64
RT = 2
RH = 7
RW = 7
PAD = 8
BR = 8
NHG = 4
BF = jnp.bfloat16
F32 = jnp.float32


def dot_nn(a, b):
    return jnp.dot(a, b, preferred_element_type=F32)


def dot_nt(a, b):
    return lax.dot_general(a, b, (((1,), (1,)), ((), ())), preferred_element_type=F32)


def stack_heads(a, mask_ref):
    return (a[None] * mask_ref[...]).reshape(NHG * a.shape[0], a.shape[1])


def pick_heads(a):
    n = a.shape[0] // NHG
    head = lax.broadcasted_iota(jnp.int32, (n, a.shape[1]), 1) // HD
    out = a[:n]
    for h in range(1, NHG):
        out = jnp.where(head == h, a[h * n : (h + 1) * n], out)
    return out


def make_bias(block, dims):
    frames, rows, cols, slots, tm_size, height_size = dims
    t = lax.axis_index("tm")
    first = lax.axis_index("height") * rows
    span = (BR + 2 * PAD) * cols
    own = BR * cols
    shape = (frames * own, slots * span)
    i = lax.broadcasted_iota(jnp.int32, shape, 0)
    j = lax.broadcasted_iota(jnp.int32, shape, 1)
    qf = t * frames + i // own
    qr = (i % own) // cols
    slot = j // span
    kr = (j % span) // cols
    group = slot // frames
    if slots == 2 * frames:
        base = jnp.where(group == 0, t, 1 - t)
    else:
        base = jnp.where(group == 0, t, jnp.where(group == 1, t - 1, t + 1))
    kf = base * frames + slot % frames
    near = (jnp.abs(kf - qf) <= RT) & (jnp.abs(kr - PAD - qr) <= RH)
    row = first + block * BR + kr - PAD
    real = (kf >= 0) & (kf < tm_size * frames) & (row >= 0) & (row < height_size * rows)
    return jnp.where(near & real, 0.0, -1e30).astype(F32)


def forward_rows(b, dims, q_ref, k_ref, v_ref, g_ref, mixed_ref, dq_ref, bias, mask_ref):
    frames, rows, cols, slots, _, _ = dims
    own = BR * cols
    span = (BR + 2 * PAD) * cols
    width = NHG * HD
    count = k_ref.shape[2] // width
    n = frames * own
    mine = pl.ds(pl.multiple_of((b + 1) * own, own), own)
    inner = pl.ds(pl.multiple_of(b * own, own), own)
    wide = pl.ds(pl.multiple_of(b * own, own), span)
    state = {}

    def scores(g):
        at = pl.ds(g * width, width)
        q = stack_heads(q_ref[:frames, mine, at].reshape(n, width), mask_ref)
        gr = stack_heads(g_ref[:frames, mine, at].reshape(n, width), mask_ref)
        k = k_ref[:, wide, at].reshape(slots * span, width)
        v = v_ref[:, wide, at].reshape(slots * span, width)
        state[g] = [gr, dot_nt(q, k), dot_nt(gr, v)]

    def soft(g):
        s = state[g][1]
        s = (s.reshape(NHG, n, slots * span) + bias[None]).reshape(NHG * n, slots * span)
        top = jnp.max(s, axis=1, keepdims=True)
        e = jnp.exp(s - top)
        total = jnp.sum(e, axis=1, keepdims=True)
        state[g] += [e * (1.0 / total), top + jnp.log(total)]

    def mix(g):
        at = pl.ds(g * width, width)
        v = v_ref[:, wide, at].reshape(slots * span, width)
        mixed = dot_nn(state[g][3].astype(BF), v).astype(BF)
        state[g].append(mixed)
        mixed_ref[:, inner, at] = pick_heads(mixed).reshape(frames, own, width)

    def grads(g, stat):
        at = pl.ds(g * width, width)
        gr, _, dp, p, lse, mixed = state.pop(g)
        delta = jnp.sum(gr.astype(F32) * mixed.astype(F32), axis=1, keepdims=True)
        ds = (p * (dp - delta)).astype(BF)
        k = k_ref[:, wide, at].reshape(slots * span, width)
        dq = pick_heads(dot_nn(ds, k)) * HD ** (-0.5)
        dq_ref[:, inner, at] = dq.astype(BF).reshape(frames, own, width)
        lane = lax.broadcasted_iota(jnp.int32, (n, 128), 1)
        for h in range(NHG):
            stat = jnp.where(lane == g * NHG + h, lse[h * n : (h + 1) * n], stat)
            stat = jnp.where(lane == 64 + g * NHG + h, delta[h * n : (h + 1) * n], stat)
        return stat

    stat = jnp.zeros((n, 128), F32)
    scores(0)
    scores(1)
    soft(0)
    for g in range(count):
        if g + 2 < count:
            scores(g + 2)
        mix(g)
        if g + 1 < count:
            soft(g + 1)
        stat = grads(g, stat)
    return stat.reshape(frames, own, 128)


def backward_rows(b, dims, q_ref, k_ref, v_ref, g_ref, dk_ref, dv_ref, flip, bias, mask_ref):
    frames, rows, cols, slots, _, _ = dims
    own = BR * cols
    span = (BR + 2 * PAD) * cols
    width = NHG * HD
    count = k_ref.shape[2] // width
    n = frames * own
    full = (NHG, n, slots * span)
    mine = pl.ds(pl.multiple_of((b + 1) * own, own), own)
    inner = pl.ds(pl.multiple_of(b * own, own), own)
    wide = pl.ds(pl.multiple_of(b * own, own), span)
    state = {}

    def scores(g):
        at = pl.ds(g * width, width)
        k = stack_heads(k_ref[:frames, mine, at].reshape(n, width), mask_ref)
        v = stack_heads(v_ref[:frames, mine, at].reshape(n, width), mask_ref)
        q = q_ref[:, wide, at].reshape(slots * span, width)
        gr = g_ref[:, wide, at].reshape(slots * span, width)
        state[g] = [dot_nt(k, q), dot_nt(v, gr)]

    def soft(g):
        s, dp = state[g]
        lse = flip[g * NHG : (g + 1) * NHG, :]
        delta = flip[64 + g * NHG : 64 + (g + 1) * NHG, :]
        p = jnp.exp(s.reshape(full) + bias[None] - lse[:, None, :])
        ds = p * (dp.reshape(full) - delta[:, None, :])
        state[g] = [p.astype(BF).reshape(NHG * n, -1), ds.astype(BF).reshape(NHG * n, -1)]

    def grads(g):
        at = pl.ds(g * width, width)
        p, ds = state.pop(g)
        q = q_ref[:, wide, at].reshape(slots * span, width)
        gr = g_ref[:, wide, at].reshape(slots * span, width)
        dv_ref[:, inner, at] = pick_heads(dot_nn(p, gr)).astype(BF).reshape(frames, own, width)
        dk_ref[:, inner, at] = pick_heads(dot_nn(ds, q)).astype(BF).reshape(frames, own, width)

    scores(0)
    scores(1)
    soft(0)
    for g in range(count):
        if g + 2 < count:
            scores(g + 2)
        if g + 1 < count:
            soft(g + 1)
        grads(g)


def project(jobs):
    width = jobs[0][3].shape[0]
    tile = 256

    def step(i, _):
        at = pl.ds(pl.multiple_of(i * tile, tile), tile)
        for src_ref, (first, count), spans, w_ref, dst_ref, flip, factor in jobs:
            some = pl.ds(first, count)
            parts = [src_ref[some, a : a + size, :].reshape(count * size, width) for a, size in spans]
            rows = parts[0] if len(parts) == 1 else jnp.concatenate(parts, axis=0)
            out = dot_nt(rows, w_ref[at, :]) if flip else dot_nn(rows, w_ref[:, at])
            out = out.astype(BF)
            if factor != 1:
                out = out * jnp.asarray(factor, BF)
            begin = 0
            for a, size in spans:
                piece = out[begin : begin + count * size]
                if len(dst_ref.shape) == 4:
                    dst_ref[some, :, :, at] = piece.reshape(count, *dst_ref.shape[1:3], tile)
                else:
                    dst_ref[some, a : a + size, at] = piece.reshape(count, size, tile)
                begin += count * size
        return 0

    lax.fori_loop(0, width // tile, step, 0)


class Exchange:
    def __init__(self, ref, sems, dims, edge):
        frames, rows, cols, slots, tm, height = dims
        self.ref, self.edge, self.frames = ref, edge, frames
        self.t, self.h = lax.axis_index("tm"), lax.axis_index("height")
        self.tm, self.height = tm, height
        self.send_x, self.recv_x, self.send_h, self.recv_h = sems
        tokens = rows * cols
        self.pieces = [(edge, edge), (tokens, edge), (2 * edge, tokens - 2 * edge)]
        self.groups = slots // frames

    def links(self):
        if self.tm == 2:
            return [(1, 1 - self.t, None, None)]
        return [
            (1, self.t + 1, self.t < self.tm - 1, self.t > 0),
            (2, self.t - 1, self.t > 0, self.t < self.tm - 1),
        ]

    def tm_copy(self, link, piece):
        group, target, _, _ = self.links()[link]
        start, size = self.pieces[piece]
        rows = pl.ds(start, size)
        return pltpu.make_async_remote_copy(
            src_ref=self.ref.at[pl.ds(0, self.frames), rows],
            dst_ref=self.ref.at[pl.ds(group * self.frames, self.frames), rows],
            send_sem=self.send_x.at[link * 3 + piece],
            recv_sem=self.recv_x.at[link * 3 + piece],
            device_id=(target, self.h),
            device_id_type=pl.DeviceIdType.MESH,
        )

    def row_copy(self, group, up):
        low, high = self.pieces[0][0], self.pieces[1][0]
        end = high + self.edge
        some = pl.ds(group * self.frames, self.frames)
        src, dst = (high, 0) if up else (low, end)
        slot = group * 2 + int(up)
        return pltpu.make_async_remote_copy(
            src_ref=self.ref.at[some, pl.ds(src, self.edge)],
            dst_ref=self.ref.at[some, pl.ds(dst, self.edge)],
            send_sem=self.send_h.at[slot],
            recv_sem=self.recv_h.at[slot],
            device_id=(self.t, self.h + 1 if up else self.h - 1),
            device_id_type=pl.DeviceIdType.MESH,
        )

    def when(self, cond, act):
        if cond is None:
            act()
        else:
            pl.when(cond)(act)

    def clear(self):
        low, end = self.edge, self.pieces[1][0] + self.edge
        shape = self.ref.shape

        @pl.when(self.h == 0)
        def _():
            self.ref[:, 0:low, :] = jnp.zeros((shape[0], low, shape[2]), self.ref.dtype)

        @pl.when(self.h == self.height - 1)
        def _():
            self.ref[:, end:, :] = jnp.zeros((shape[0], low, shape[2]), self.ref.dtype)

        for group, _, _, there in self.links():
            if there is not None:

                @pl.when(jnp.logical_not(there))
                def _(group=group):
                    some = pl.ds(group * self.frames, self.frames)
                    self.ref[some, low:end, :] = jnp.zeros((self.frames, end - low, shape[2]), self.ref.dtype)

    def there(self, group):
        return None if group == 0 else self.links()[group - 1][3]

    def both(self, a, b):
        return b if a is None else a & b

    def send_tm(self):
        for piece in range(3):
            for link, (_, _, sends, _) in enumerate(self.links()):
                self.when(sends, lambda link=link, piece=piece: self.tm_copy(link, piece).start())

    def got_tm(self, pieces):
        for link, (_, _, _, gets) in enumerate(self.links()):
            for piece in pieces:
                self.when(gets, lambda link=link, piece=piece: self.tm_copy(link, piece).wait_recv())

    def send_rows(self, groups):
        for group in groups:
            there = self.there(group)
            self.when(self.both(there, self.h < self.height - 1), lambda g=group: self.row_copy(g, True).start())
            self.when(self.both(there, self.h > 0), lambda g=group: self.row_copy(g, False).start())

    def got_rows(self, groups):
        for group in groups:
            there = self.there(group)
            self.when(self.both(there, self.h > 0), lambda g=group: self.row_copy(g, True).wait_recv())
            self.when(self.both(there, self.h < self.height - 1), lambda g=group: self.row_copy(g, False).wait_recv())

    def sent(self):
        for piece in range(3):
            for link, (_, _, sends, _) in enumerate(self.links()):
                self.when(sends, lambda link=link, piece=piece: self.tm_copy(link, piece).wait_send())
        for group in range(self.groups):
            there = self.there(group)
            self.when(self.both(there, self.h < self.height - 1), lambda g=group: self.row_copy(g, True).wait_send())
            self.when(self.both(there, self.h > 0), lambda g=group: self.row_copy(g, False).wait_send())


def greet(dims):
    _, _, _, _, tm, height = dims
    t, h = lax.axis_index("tm"), lax.axis_index("height")
    barrier = pltpu.get_barrier_semaphore()
    count = jnp.int32(0)
    others = [(h > 0, t, h - 1), (h < height - 1, t, h + 1)]
    if tm == 2:
        pl.semaphore_signal(barrier, inc=1, device_id=(1 - t, h), device_id_type=pl.DeviceIdType.MESH)
        count = count + 1
    else:
        others += [(t > 0, t - 1, h), (t < tm - 1, t + 1, h)]
    for cond, tt, hh in others:

        @pl.when(cond)
        def _(tt=tt, hh=hh):
            pl.semaphore_signal(barrier, inc=1, device_id=(tt, hh), device_id_type=pl.DeviceIdType.MESH)

        count = count + cond.astype(jnp.int32)
    return count


def kernel(
    dims, x_hbm, go_hbm, wq_hbm, wk_hbm, wv_hbm, wo_hbm,
    attended_hbm, out_hbm,
    attended_ref, out_ref, x_ref, go_ref, q_ref, k_ref, v_ref, g_ref, wq_ref, wk_ref, wv_ref, wo_ref,
    mixed_ref, dq_ref, dk_ref, dv_ref, stat_ref, bias_ref, x4_ref, go4_ref, mask_ref, local_sem,
    *sems,
):
    frames, rows, cols, slots, tm, height = dims
    width = x_ref.shape[2]
    own = BR * cols
    span = (BR + 2 * PAD) * cols
    edge = PAD * cols
    tokens = rows * cols
    blocks = rows // BR
    scale = HD ** (-0.5)
    mid = pl.ds(edge, tokens)
    loads = [
        pltpu.make_async_copy(x_hbm, x4_ref, local_sem.at[0]),
        pltpu.make_async_copy(go_hbm, go4_ref, local_sem.at[1]),
        pltpu.make_async_copy(wq_hbm, wq_ref, local_sem.at[2]),
        pltpu.make_async_copy(wk_hbm, wk_ref, local_sem.at[3]),
        pltpu.make_async_copy(wv_hbm, wv_ref, local_sem.at[4]),
        pltpu.make_async_copy(wo_hbm, wo_ref, local_sem.at[5]),
    ]
    for load in loads:
        load.start()
    ex_x = Exchange(x_ref, sems[0:4], dims, edge)
    ex_go = Exchange(go_ref, sems[4:8], dims, edge)
    ex_st = Exchange(stat_ref, sems[8:12], dims, edge)
    count = greet(dims)
    loads[0].wait()
    x_ref[pl.ds(0, frames), mid, :] = x4_ref[...].reshape(frames, tokens, width)
    pl.semaphore_wait(pltpu.get_barrier_semaphore(), count)
    ex_x.send_tm()
    ex_x.send_rows([0])
    loads[1].wait()
    go_ref[pl.ds(0, frames), mid, :] = go4_ref[...].reshape(frames, tokens, width)
    ex_go.send_rows([0])
    ex_x.clear()
    ex_go.clear()
    ex_st.clear()

    def fill(b, _):
        bias_ref[b] = make_bias(b, dims)
        return 0

    lax.fori_loop(0, blocks, fill, 0)
    head = lax.broadcasted_iota(jnp.int32, mask_ref.shape, 2) // HD
    mask_ref[...] = (head == lax.broadcasted_iota(jnp.int32, mask_ref.shape, 0)).astype(F32).astype(BF)
    centre = [(edge, tokens)]
    rims = [(0, edge), (edge + tokens, edge)]
    for load in loads[2:]:
        load.wait()

    def to_q(slots, spans):
        return (x_ref, slots, spans, wq_ref, q_ref, False, scale)

    def to_k(slots, spans):
        return (x_ref, slots, spans, wk_ref, k_ref, False, 1)

    def to_v(slots, spans):
        return (x_ref, slots, spans, wv_ref, v_ref, False, 1)

    def to_g(slots, spans):
        return (go_ref, slots, spans, wo_ref, g_ref, True, 1)

    first = (0, frames)
    rest = (frames, slots - frames)
    project([make(first, centre) for make in (to_q, to_k, to_v, to_g)])
    ex_x.got_rows([0])
    ex_go.got_rows([0])
    project([make(first, rims) for make in (to_q, to_k, to_v, to_g)])

    def forward(b):
        stat = forward_rows(b, dims, q_ref, k_ref, v_ref, g_ref, mixed_ref, dq_ref, bias_ref[b], mask_ref)
        at = pl.ds(pl.multiple_of((b + 1) * own, own), own)
        stat_ref[pl.ds(0, frames), at, :] = stat

    def backward(b):
        at = pl.ds(pl.multiple_of(b * own, own), span)
        flip = stat_ref[:, at, :].reshape(slots * span, 128).T
        backward_rows(b, dims, q_ref, k_ref, v_ref, g_ref, dk_ref, dv_ref, flip, bias_ref[b], mask_ref)

    def inner_blocks(act):
        def step(b, _):
            act(b)
            return 0

        lax.fori_loop(1, blocks - 1, step, 0)

    def outer_blocks(act):
        def step(i, _):
            act(i * (blocks - 1))
            return 0

        lax.fori_loop(0, 2, step, 0)

    others = list(range(1, slots // frames))
    ex_x.got_tm([0, 1])
    ex_x.send_rows(others)
    edges = [(edge, edge), (tokens, edge)]
    project([to_k(rest, edges), to_v(rest, edges)])
    ex_x.got_tm([2])
    ex_go.send_tm()
    ex_x.got_rows(others)
    left = [(2 * edge, tokens - 2 * edge)] + rims
    project([to_k(rest, left), to_v(rest, left)])
    inner_blocks(forward)
    ex_go.got_tm([0, 1])
    ex_go.send_rows(others)
    outer_blocks(forward)
    ex_st.send_tm()
    ex_st.send_rows([0])
    ex_go.got_tm([2])
    ex_go.got_rows(others)
    project([
        to_q(rest, centre + rims),
        to_g(rest, centre + rims),
        (mixed_ref, first, [(0, tokens)], wo_ref, attended_ref, False, 1),
    ])
    ex_st.got_tm([0, 1])
    ex_st.send_rows(others)
    attended_copy = pltpu.make_async_copy(attended_ref, attended_hbm, local_sem.at[6])
    attended_copy.start()
    ex_st.got_tm([2])
    inner_blocks(backward)
    ex_st.got_rows([0] + others)
    outer_blocks(backward)
    tile = 256

    def out_copy(i):
        at = (slice(None), slice(None), slice(None), pl.ds(pl.multiple_of(i * tile, tile), tile))
        return pltpu.make_async_copy(out_ref.at[at], out_hbm.at[at], local_sem.at[7 + i])

    def out_step(i, _):
        at = pl.ds(pl.multiple_of(i * tile, tile), tile)
        total = dot_nt(dq_ref[...].reshape(frames * tokens, width), wq_ref[at, :])
        total += dot_nt(dk_ref[...].reshape(frames * tokens, width), wk_ref[at, :])
        total += dot_nt(dv_ref[...].reshape(frames * tokens, width), wv_ref[at, :])
        out_ref[:, :, :, at] = total.astype(BF).reshape(frames, rows, cols, tile)
        out_copy(i).start()
        return 0

    lax.fori_loop(0, width // tile, out_step, 0)
    ex_x.sent()
    ex_go.sent()
    ex_st.sent()
    attended_copy.wait()
    for i in range(width // tile):
        out_copy(i).wait()


def copy_kernel(a_hbm, b_hbm, a_out, b_out, held_ref, in_sem, out_sem):
    arrive, leave = [], []
    for i, (src, dst) in enumerate(((a_hbm, a_out), (b_hbm, b_out))):
        for f in range(src.shape[0]):
            slot = i * src.shape[0] + f
            arrive.append(pltpu.make_async_copy(src.at[f], held_ref.at[slot], in_sem.at[slot]))
            leave.append(pltpu.make_async_copy(held_ref.at[slot], dst.at[f], out_sem.at[slot]))
    for copy in arrive:
        copy.start()
    for before, after in zip(arrive, leave):
        before.wait()
        after.start()
    for copy in leave:
        copy.wait()


def shards(inputs, w_query, w_key, w_value, w_out, grad_out):
    frames, rows, cols, width = inputs.shape
    tm, height = lax.axis_size("tm"), lax.axis_size("height")
    groups = 2 if tm == 2 else 3
    slots = groups * frames
    dims = (frames, rows, cols, slots, tm, height)
    tokens = rows * cols
    wide = tokens + 2 * PAD * cols
    keys = slots * (BR + 2 * PAD) * cols
    mine = frames * BR * cols
    hbm = pl.BlockSpec(memory_space=pl.ANY)
    links = 3 * (groups - 1)
    sems = [pltpu.SemaphoreType.DMA((links,))] * 2 + [pltpu.SemaphoreType.DMA((2 * groups,))] * 2
    both = pl.pallas_call(
        functools.partial(kernel, dims),
        out_shape=[jax.ShapeDtypeStruct(inputs.shape, BF)] * 2,
        in_specs=[hbm] * 6,
        out_specs=[hbm] * 2,
        scratch_shapes=[pltpu.VMEM(inputs.shape, BF)] * 2
        + [pltpu.VMEM((slots, wide, width), BF)] * 6
        + [pltpu.VMEM((width, width), BF)] * 4
        + [pltpu.VMEM((frames, tokens, width), BF)] * 4
        + [
            pltpu.VMEM((slots, wide, 128), F32),
            pltpu.VMEM((rows // BR, mine, keys), F32),
            pltpu.VMEM(inputs.shape, BF),
            pltpu.VMEM(inputs.shape, BF),
            pltpu.VMEM((NHG, mine, NHG * HD), BF),
            pltpu.SemaphoreType.DMA((7 + width // 256,)),
        ]
        + sems * 3,
        compiler_params=pltpu.CompilerParams(
            vmem_limit_bytes=56 * 1024 * 1024, collective_id=0, has_side_effects=True
        ),
        name="attention",
    )(inputs, grad_out, w_query, w_key, w_value, w_out)
    return pl.pallas_call(
        copy_kernel,
        out_shape=[jax.ShapeDtypeStruct(inputs.shape, BF)] * 2,
        in_specs=[hbm] * 2,
        out_specs=[hbm] * 2,
        scratch_shapes=[
            pltpu.VMEM((2 * frames, rows, cols, width), BF),
            pltpu.SemaphoreType.DMA((2 * frames,)),
            pltpu.SemaphoreType.DMA((2 * frames,)),
        ],
        name="copy_out",
    )(*both)


def solution(mesh):
    placed = (P("tm", "height", None, None), P(), P(), P(), P(), P("tm", "height", None, None))
    return jax.shard_map(
        shards,
        mesh=mesh,
        in_specs=placed,
        out_specs=(P("tm", "height", None, None), P("tm", "height", None, None)),
        check_vma=False,
    )
```
